768 devices in a mesh: wide: 48 (over z_lo, y), grp: 16 (over z_hi, x, core).
Axes of the slice: x: 4, y: 8, z: 12 (z_hi: 2, z_lo: 6; z = z_hi * 6 + z_lo), core: 2. Of those that a mesh axis runs over, the one named last changes fastest.
Arguments:
- pooled: bfloat16 [6144, 49152], P(None, ('wide', 'grp')), may hold values from -6 to 6
- owner_order: int32 [256], replicated, may hold values from 0 to 255, each once
- fm_proj: bfloat16 [2, 256, 32], replicated, may hold values from -0.375 to 0.375
- fm_mix: bfloat16 [2, 128, 256], replicated, may hold values from -0.375 to 0.375
- fm_out: bfloat16 [2, 32, 192], replicated, may hold values from -0.078125 to 0.078125
- lcb_weight: bfloat16 [2, 128, 256], replicated, may hold values from -0.375 to 0.375
- gain: float32 [2, 192], replicated, may hold values from 0.5 to 1.5
- cotangent: bfloat16 [6144, 49152], P(('wide', 'grp')), may hold values from -6 to 6
Outputs:
- layer_out: bfloat16 [6144, 49152], P(('wide', 'grp'))
- d_pooled: bfloat16 [6144, 49152], P(None, ('wide', 'grp'))
- grad_fm_proj: float32 [2, 256, 32], replicated
- grad_fm_mix: float32 [2, 128, 256], replicated
- grad_fm_out: float32 [2, 32, 192], replicated
- grad_lcb: float32 [2, 128, 256], replicated
- grad_gain: float32 [2, 192], replicated
The draws below stay inside these ranges and needn't reach their ends.
Inputs may be any that keep to these rules, and one draw needn't show every extreme that they name: `owner_order`: each feature stands in exactly one slot.
All inputs are finite; a program needn't handle non-finite values.
Results may differ from the reference program's by a relative error of at most 0.019.
Values may be sent and summed in bfloat16 or wider, within the bound.
A program may use at most 32 MiB of HBM per device.

```python
import jax
import jax.numpy as jnp
from jax import lax

F = 256
E = 192
K = 32
NF = 128
NL = 128
LAYERS = 2
SAMPLES = 6144
N_WIDE = 48


def block_scale(own_key, dims, cuts, least, top_value):
    def one(dim, shards_of):
        steps = jax.random.uniform(jax.random.fold_in(jax.random.fold_in(own_key, 6), dim), (shards_of,), jnp.float32, least / len(cuts), top_value / len(cuts))
        return jnp.repeat(jnp.exp(steps), dims[dim] // shards_of).reshape((-1,) + (1,) * (len(dims) - dim - 1))

    level = one(*cuts[0])
    for cut in cuts[1:]:
        level = level * one(*cut)
    return level


def normal_values(rng, shape, deviation, limit, pieces=(), held_as=jnp.bfloat16):
    level = block_scale(rng, shape, pieces, -0.22, 0.18) if pieces else 1.0
    drawn = jax.random.normal(rng, shape, jnp.float32) * deviation * level
    return jnp.minimum(jnp.maximum(drawn, -limit), limit).astype(held_as)


def setup_inputs(seed: int = 0) -> dict:
    seeds = jax.random.split(jax.random.key(seed), 9)
    return {
        "pooled": normal_values(seeds[0], (SAMPLES, F * E), 1.0, 6.0, ((1, 768),)),
        "owner_order": jax.random.permutation(seeds[1], F).astype(jnp.int32),
        "fm_proj": normal_values(seeds[2], (LAYERS, F, K), F ** -0.5, 0.375),
        "fm_mix": normal_values(seeds[3], (LAYERS, NF, F), F ** -0.5, 0.375),
        "fm_out": normal_values(seeds[4], (LAYERS, K, E), (K * E) ** -0.5, 0.078125),
        "lcb_weight": normal_values(seeds[5], (LAYERS, NL, F), F ** -0.5, 0.375),
        "gain": jnp.clip(1.0 + 0.1 * jax.random.normal(seeds[6], (LAYERS, E), jnp.float32), 0.5, 1.5),
        "cotangent": normal_values(seeds[7], (SAMPLES, F * E), 1.0, 6.0, ((0, 768),)),
    }


def product(form, left, right):
    return jnp.einsum(form, left.astype(jnp.float32), right.astype(jnp.float32))

def layer_forward(embeds, fm_proj, fm_mix, fm_out, lcb_weight, gain):
    proj_z = product('nfe,fk->nek', embeds, fm_proj).astype(jnp.bfloat16)
    inter_m = product('nfe,nek->nfk', embeds, proj_z).astype(jnp.bfloat16)
    mix_q = product('gf,nfk->ngk', fm_mix, inter_m).astype(jnp.bfloat16)
    fm_branch = product('ngk,ke->nge', mix_q, fm_out)
    lcb_branch = product('lf,nfe->nle', lcb_weight, embeds)
    summed = jnp.concatenate([fm_branch, lcb_branch], axis=1) + embeds.astype(jnp.float32)
    center = summed - lax.optimization_barrier(jnp.mean(summed, axis=-1, keepdims=True))
    variance = lax.optimization_barrier(jnp.mean(center * center, axis=-1, keepdims=True))
    inv_std = lax.rsqrt(variance + 1e-05)
    normed = center * inv_std
    result = (normed * gain).astype(jnp.bfloat16)
    return (result, (proj_z, inter_m, mix_q, normed, inv_std))

def layer_backward(embeds, cot_rows, saved, fm_proj, fm_mix, fm_out, lcb_weight, gain):
    proj_z, inter_m, mix_q, normed, inv_std = saved
    split = fm_mix.shape[0]
    cot_float = cot_rows.astype(jnp.float32)
    grad_gain = lax.optimization_barrier(jnp.sum(cot_float * normed, axis=(0, 1)))
    d_norm = cot_float * gain
    grad_sum = inv_std * (d_norm - lax.optimization_barrier(jnp.mean(d_norm, axis=-1, keepdims=True)) - normed * lax.optimization_barrier(jnp.mean(d_norm * normed, axis=-1, keepdims=True)))
    grad_sum = grad_sum.astype(jnp.bfloat16)
    d_fm_rows = grad_sum[:, :split]
    d_lcb_rows = grad_sum[:, split:]
    grad_lcb = product('nle,nfe->lf', d_lcb_rows, embeds)
    grad_fm_out = product('ngk,nge->ke', mix_q, d_fm_rows)
    grad_mix_q = product('nge,ke->ngk', d_fm_rows, fm_out).astype(jnp.bfloat16)
    grad_fm_mix = product('ngk,nfk->gf', grad_mix_q, inter_m)
    grad_inter = product('gf,ngk->nfk', fm_mix, grad_mix_q).astype(jnp.bfloat16)
    grad_proj_z = product('nfe,nfk->nek', embeds, grad_inter).astype(jnp.bfloat16)
    grad_fm_proj = product('nfe,nek->fk', embeds, grad_proj_z)
    grad_embeds = (grad_sum.astype(jnp.float32) + product('lf,nle->nfe', lcb_weight, d_lcb_rows) + product('nfk,nek->nfe', grad_inter, proj_z) + product('fk,nek->nfe', fm_proj, grad_proj_z)).astype(jnp.bfloat16)
    return (grad_embeds, (grad_fm_proj, grad_fm_mix, grad_fm_out, grad_lcb, grad_gain))

def run_layers(embeds, cot_rows, fm_proj, fm_mix, fm_out, lcb_weight, gain):
    depth = fm_proj.shape[0]
    inputs = []
    saves = []
    current = embeds
    for layer in range(depth):
        inputs.append(current)
        current, saved = layer_forward(current, fm_proj[layer], fm_mix[layer], fm_out[layer], lcb_weight[layer], gain[layer])
        saves.append(saved)
    back = cot_rows
    grad_list = [None] * depth
    for layer in reversed(range(depth)):
        back, grads = layer_backward(inputs[layer], back, saves[layer], fm_proj[layer], fm_mix[layer], fm_out[layer], lcb_weight[layer], gain[layer])
        grad_list[layer] = grads
    stacked = tuple((jnp.stack([entry[which] for entry in grad_list]) for which in range(5)))
    return (current, back, stacked)

def reference(pooled, owner_order, fm_proj, fm_mix, fm_out, lcb_weight, gain, cotangent):
    position = jnp.zeros((F,), jnp.int32).at[owner_order].set(jnp.arange(F, dtype=jnp.int32))
    block_rows = SAMPLES // N_WIDE
    pooled_blocks = pooled.reshape(N_WIDE, block_rows, F, E)
    cot_blocks = cotangent.reshape(N_WIDE, block_rows, F, E)

    def visit(totals, pair):
        owner_rows, cot_rows = pair
        embeds = jnp.take(owner_rows, position, axis=1)
        result, grad_embeds, grads = run_layers(embeds, cot_rows, fm_proj, fm_mix, fm_out, lcb_weight, gain)
        back_rows = jnp.take(grad_embeds, owner_order, axis=1)
        merged = tuple((left + right for left, right in zip(totals, grads)))
        return (merged, (result.reshape(block_rows, F * E), back_rows.reshape(block_rows, F * E)))
    start = (jnp.zeros((LAYERS, F, K), jnp.float32), jnp.zeros((LAYERS, NF, F), jnp.float32), jnp.zeros((LAYERS, K, E), jnp.float32), jnp.zeros((LAYERS, NL, F), jnp.float32), jnp.zeros((LAYERS, E), jnp.float32))
    totals, (outputs, backs) = lax.scan(visit, start, (pooled_blocks, cot_blocks))
    scale = 1.0 / SAMPLES
    return (outputs.reshape(SAMPLES, F * E), backs.reshape(SAMPLES, F * E), totals[0] * scale, totals[1] * scale, totals[2] * scale, totals[3] * scale, totals[4] * scale)
```

```python
import functools

import jax
import jax.numpy as jnp
from jax import lax
from jax.experimental import pallas as pl
from jax.experimental.pallas import tpu as pltpu
from jax.sharding import PartitionSpec as P

F = 256
E = 192
MESH = pl.DeviceIdType.MESH
BF16 = jnp.bfloat16
F32 = jnp.float32


class Torus:
    def __init__(self, z_lo, y, z_hi, x):
        self.z_lo, self.y, self.z_hi, self.x = z_lo, y, z_hi, x
        self.z = z_lo * z_hi
        self.flat = y * x
        self.offsets = sorted(range(y), key=lambda o: -min(o, y - o))

    def place(self):
        wide, grp = lax.axis_index("wide"), lax.axis_index("grp")
        z_lo, y = wide // self.y, wide % self.y
        z_hi, rest = grp // (2 * self.x), grp % (2 * self.x)
        return z_hi * self.z_lo + z_lo, y, rest // 2, rest % 2

    def device(self, z, y, x, core):
        z_lo, z_hi = z % self.z_lo, z // self.z_lo
        return (z_lo * self.y + y, z_hi * 2 * self.x + x * 2 + core)

    def z_peer(self, z, j):
        step = (j // 2 + 1) * (1 - 2 * (j % 2))
        return (z + step + self.z) % self.z

    def flat_peer(self, y, x, j):
        spot = (y * self.x + x + 1 + j) % self.flat
        return spot // self.x, spot % self.x


def greet(torus):
    z, y, x, core = torus.place()
    barrier = pltpu.get_barrier_semaphore()

    def hello(where):
        pl.semaphore_signal(barrier, inc=1, device_id=where, device_id_type=MESH)

    hello(torus.device(z, y, x, 1 - core))

    def along_z(j, _):
        hello(torus.device(torus.z_peer(z, j), y, x, core))
        return 0

    def along_flat(j, _):
        y_to, x_to = torus.flat_peer(y, x, j)
        hello(torus.device(z, y_to, x_to, core))
        return 0

    lax.fori_loop(0, torus.z - 1, along_z, 0)
    lax.fori_loop(0, torus.flat - 1, along_flat, 0)
    pl.semaphore_wait(barrier, torus.z + torus.flat - 1)


def remote(src, dst, send, recv, where):
    return pltpu.make_async_remote_copy(
        src_ref=src, dst_ref=dst, send_sem=send, recv_sem=recv, device_id=where, device_id_type=MESH
    )


def take(ref, sem):
    pltpu.make_async_copy(ref, ref, sem).wait()


def send_z(torus, i, src, middle, z_send, z_recv):
    z, y, x, core = torus.place()
    y_to = (y + torus.offsets[i]) % torus.y
    landing = middle.at[z % torus.z_lo, z // torus.z_lo, y_to]
    pltpu.make_async_copy(src.at[z % torus.z_lo, y_to, z // torus.z_lo], landing, z_recv.at[i]).start()

    def step(j, _):
        z_to = torus.z_peer(z, j)
        block = src.at[z_to % torus.z_lo, y_to, z_to // torus.z_lo]
        remote(block, landing, z_send, z_recv.at[i], torus.device(z_to, y, x, core)).start()
        return 0

    lax.fori_loop(0, torus.z - 1, step, 0)


def send_flat(torus, i, middle, out, f_send, f_recv, z_recv):
    z, y, x, core = torus.place()
    y_to = (y + torus.offsets[i]) % torus.y
    take(middle.at[:, :, y_to], z_recv.at[i])
    for dx in range(torus.x):
        x_to = (x + dx) % torus.x
        block = middle.at[:, :, y_to, x_to]
        if torus.offsets[i] == 0 and dx == 0:
            pltpu.make_async_copy(block, out(y, x), f_recv.at[i]).start()
        else:
            remote(block, out(y, x), f_send, f_recv.at[i], torus.device(z, y_to, x_to, core)).start()


def take_sent(torus, spare, z_send, f_send):
    take(spare.at[pl.ds(0, (torus.z - 1) * torus.y * torus.x)], z_send)
    take(spare.at[pl.ds(0, (torus.flat - 1) * torus.z)], f_send)


def forward_kernel(torus, p_ref, r_ref, inbox, src, middle, spare, c_send, c_recv, z_send, z_recv, f_send, f_recv):
    z, y, x, core = torus.place()
    greet(torus)
    mate = torus.device(z, y, x, 1 - core)
    swaps = []
    for i in range(torus.y):
        y_to = (y + torus.offsets[i]) % torus.y
        swap = remote(
            p_ref.at[:, y_to, :, :, 1 - core], inbox.at[:, y_to], c_send.at[i], c_recv.at[i], mate
        )
        swap.start()
        swaps.append(swap)
    lanes = lax.broadcasted_iota(jnp.int32, (torus.x, 8, 128), 2)
    mine = (lanes // 64) == core
    for i in range(torus.y):
        y_to = (y + torus.offsets[i]) % torus.y
        swaps[i].wait_recv()

        def merge(k, _):
            z_lo, z_hi = k // torus.z_hi, k % torus.z_hi
            own = p_ref[z_lo, y_to, z_hi, :, core].astype(F32)
            other = inbox[z_lo, y_to, z_hi].astype(F32)
            src[z_lo, y_to, z_hi] = jnp.where(mine, own, other).astype(BF16)
            return 0

        lax.fori_loop(0, torus.z, merge, 0)
        send_z(torus, i, src, middle, z_send, z_recv)
    for i in range(torus.y):
        send_flat(torus, i, middle, lambda y, x: r_ref.at[:, y, :, x], f_send, f_recv, z_recv)
    for i in range(torus.y):
        y_from = (y - torus.offsets[i] + torus.y) % torus.y
        take(r_ref.at[:, y_from], f_recv.at[i])
    for i in range(torus.y):
        swaps[i].wait_send()
    take_sent(torus, spare, z_send, f_send)


def spare_shape(torus):
    return pltpu.VMEM((max((torus.z - 1) * torus.y * torus.x, (torus.flat - 1) * torus.z), 8, 128), BF16)


def forward_exchange(torus, pooled):
    doubled = jnp.concatenate([pooled, pooled], axis=1)
    doubled = doubled.reshape(torus.z_lo, torus.y, torus.z_hi, torus.x, 2, 8, 128)
    shape = (torus.z_lo, torus.y, torus.z_hi, torus.x, 8, 128)
    middle = (torus.z_lo, torus.z_hi, torus.y, torus.x, 8, 128)
    dma = pltpu.SemaphoreType.DMA
    landed = pl.pallas_call(
        functools.partial(forward_kernel, torus),
        out_shape=jax.ShapeDtypeStruct(shape, BF16),
        in_specs=[pl.BlockSpec(memory_space=pltpu.VMEM)],
        out_specs=pl.BlockSpec(memory_space=pltpu.VMEM),
        scratch_shapes=[
            pltpu.VMEM(shape, BF16),
            pltpu.VMEM(shape, BF16),
            pltpu.VMEM(middle, BF16),
            spare_shape(torus),
            dma((torus.y,)),
            dma((torus.y,)),
            dma,
            dma((torus.y,)),
            dma,
            dma((torus.y,)),
        ],
        compiler_params=pltpu.CompilerParams(
            collective_id=0, has_side_effects=True, vmem_limit_bytes=40 * 1024 * 1024
        ),
        name="forward_exchange",
    )(doubled)
    chips = torus.z * torus.flat
    return landed.reshape(chips, 8, 128).transpose(1, 0, 2).reshape(8, chips * 128)


def backward_kernel(
    torus, b_ref, g_ref, d_ref, t_ref, middle, spare, g_spare, g_inbox, g_half, g_parts, g_own, g_rings, g_done, g_full,
    c_send, c_recv, z_send, z_recv, f_send, f_recv,
    a_send, a_recv, s_send, s_recv, k_send, k_recv, w_send, w_recv, e_send, e_recv,
):
    z, y, x, core = torus.place()
    greet(torus)
    mate = torus.device(z, y, x, 1 - core)
    z_lo, z_hi = z % torus.z_lo, z // torus.z_lo

    first = remote(g_ref.at[1 - core], g_inbox, a_send, a_recv, mate)
    first.start()
    for i in range(torus.y):
        send_z(torus, i, b_ref, middle, z_send, z_recv)

    def to_flat(block, landing, send, recv):
        def step(j, _):
            y_to, x_to = torus.flat_peer(y, x, j)
            remote(block(y_to, x_to), landing, send, recv, torus.device(z, y_to, x_to, core)).start()
            return 0

        pltpu.make_async_copy(block(y, x), landing, recv).start()
        lax.fori_loop(0, torus.flat - 1, step, 0)

    def sum_pair():
        first.wait_recv()

        def add(k, _):
            own = g_ref[core, k].astype(F32)
            g_half[k] = (own + g_inbox[k].astype(F32)).astype(BF16)
            return 0

        lax.fori_loop(0, torus.y, add, 0)
        to_flat(lambda y_to, x_to: g_half.at[y_to, x_to], g_parts.at[y, x], s_send, s_recv)

    def sum_flat():
        take(g_parts, s_recv)

        def add(k, total):
            return total + jnp.sum(g_parts[k].astype(F32), axis=0)

        g_own[...] = lax.fori_loop(0, torus.y, add, jnp.zeros((16, 256), F32)).astype(BF16)
        landing = g_rings.at[z]
        pltpu.make_async_copy(g_own, landing, k_recv).start()

        def step(j, _):
            z_to = torus.z_peer(z, j)
            remote(g_own, landing, k_send, k_recv, torus.device(z_to, y, x, core)).start()
            return 0

        lax.fori_loop(0, torus.z - 1, step, 0)

    def sum_ring():
        take(g_rings, k_recv)

        def add(k, total):
            return total + g_rings[k].astype(F32)

        g_done[...] = lax.fori_loop(0, torus.z, add, jnp.zeros((16, 256), F32)).astype(BF16)
        to_flat(lambda y_to, x_to: g_done, g_full.at[y, x], w_send, w_recv)

    last = remote(g_full, t_ref.at[core], e_send, e_recv, mate)

    def share_pair():
        take(g_full, w_recv)
        last.start()
        t_ref[core] = g_full[...]

    between = {0: sum_pair, 2: sum_flat, 4: sum_ring, 6: share_pair}
    if torus.y < 8:
        between = {}
    swaps = []
    for i in range(torus.y):
        if i in between:
            between[i]()
        send_flat(torus, i, middle, lambda y, x: d_ref.at[:, y, :, x, core], f_send, f_recv, z_recv)
    if not between:
        for part in (sum_pair, sum_flat, sum_ring, share_pair):
            part()
    for i in range(torus.y):
        y_from = (y - torus.offsets[i] + torus.y) % torus.y
        block = d_ref.at[:, y_from, :, :, core]
        take(block, f_recv.at[i])
        swap = remote(block, block, c_send.at[i], c_recv.at[i], mate)
        swap.start()
        swaps.append(swap)
    last.wait()
    for swap in swaps:
        swap.wait()
    first.wait_send()
    take_sent(torus, spare, z_send, f_send)
    take(g_spare.at[pl.ds(0, torus.flat - 1)], s_send)
    take(g_spare.at[pl.ds(0, torus.flat - 1)], w_send)
    take(g_spare.at[pl.ds(0, torus.z - 1)], k_send)


def backward_exchange(torus, rows, grads):
    chips = torus.z * torus.flat
    blocks = rows.reshape(8, chips, 128).transpose(1, 0, 2)
    blocks = blocks.reshape(torus.z_lo, torus.y, torus.z_hi, torus.x, 8, 128)
    middle = (torus.z_lo, torus.z_hi, torus.y, torus.x, 8, 128)
    half = (torus.y, torus.x, 16, 256)
    dma = pltpu.SemaphoreType.DMA
    d_full, total = pl.pallas_call(
        functools.partial(backward_kernel, torus),
        out_shape=(
            jax.ShapeDtypeStruct((torus.z_lo, torus.y, torus.z_hi, torus.x, 2, 8, 128), BF16),
            jax.ShapeDtypeStruct((2,) + half, BF16),
        ),
        in_specs=[pl.BlockSpec(memory_space=pltpu.VMEM)] * 2,
        out_specs=[pl.BlockSpec(memory_space=pltpu.VMEM)] * 2,
        scratch_shapes=[
            pltpu.VMEM(middle, BF16),
            spare_shape(torus),
            pltpu.VMEM((max(torus.flat, torus.z) - 1, 16, 256), BF16),
            pltpu.VMEM(half, BF16),
            pltpu.VMEM(half, BF16),
            pltpu.VMEM(half, BF16),
            pltpu.VMEM((16, 256), BF16),
            pltpu.VMEM((torus.z, 16, 256), BF16),
            pltpu.VMEM((16, 256), BF16),
            pltpu.VMEM(half, BF16),
            dma((torus.y,)),
            dma((torus.y,)),
            dma,
            dma((torus.y,)),
            dma,
            dma((torus.y,)),
        ]
        + [dma] * 10,
        compiler_params=pltpu.CompilerParams(
            collective_id=1, has_side_effects=True, vmem_limit_bytes=40 * 1024 * 1024
        ),
        name="backward_exchange",
    )(blocks, grads)
    core = lax.axis_index("grp") % 2
    wide = d_full.reshape(chips * 16, 128)
    d_pooled = lax.dynamic_slice(wide, (0, core * 64), (chips * 16, 64))
    return d_pooled, total


def product(form, left, right):
    return jnp.einsum(form, left, right, preferred_element_type=F32)


def layer_forward(embeds, fm_proj, fm_mix, fm_out, lcb_weight, gain):
    proj_z = product("nfe,fk->nek", embeds, fm_proj).astype(BF16)
    inter_m = product("nfe,nek->nfk", embeds, proj_z).astype(BF16)
    mix_q = product("gf,nfk->ngk", fm_mix, inter_m).astype(BF16)
    fm_branch = product("ngk,ke->nge", mix_q, fm_out)
    lcb_branch = product("lf,nfe->nle", lcb_weight, embeds)
    summed = jnp.concatenate([fm_branch, lcb_branch], axis=1) + embeds.astype(F32)
    center = summed - jnp.mean(summed, axis=-1, keepdims=True)
    variance = jnp.mean(center * center, axis=-1, keepdims=True)
    inv_std = lax.rsqrt(variance + 1e-05)
    normed = center * inv_std
    result = (normed * gain).astype(BF16)
    return (result, (proj_z, inter_m, mix_q, normed, inv_std))


def layer_backward(embeds, cot_rows, saved, fm_proj, fm_mix, fm_out, lcb_weight, gain):
    proj_z, inter_m, mix_q, normed, inv_std = saved
    split = fm_mix.shape[0]
    cot_float = cot_rows.astype(F32)
    grad_gain = jnp.sum(cot_float * normed, axis=(0, 1))
    d_norm = cot_float * gain
    grad_sum = inv_std * (
        d_norm
        - jnp.mean(d_norm, axis=-1, keepdims=True)
        - normed * jnp.mean(d_norm * normed, axis=-1, keepdims=True)
    )
    grad_sum = grad_sum.astype(BF16)
    d_fm_rows = grad_sum[:, :split]
    d_lcb_rows = grad_sum[:, split:]
    grad_lcb = product("nle,nfe->lf", d_lcb_rows, embeds)
    grad_fm_out = product("ngk,nge->ke", mix_q, d_fm_rows)
    grad_mix_q = product("nge,ke->ngk", d_fm_rows, fm_out).astype(BF16)
    grad_fm_mix = product("ngk,nfk->gf", grad_mix_q, inter_m)
    grad_inter = product("gf,ngk->nfk", fm_mix, grad_mix_q).astype(BF16)
    grad_proj_z = product("nfe,nfk->nek", embeds, grad_inter).astype(BF16)
    grad_fm_proj = product("nfe,nek->fk", embeds, grad_proj_z)
    grad_embeds = (
        grad_sum.astype(F32)
        + product("lf,nle->nfe", lcb_weight, d_lcb_rows)
        + product("nfk,nek->nfe", grad_inter, proj_z)
        + product("fk,nek->nfe", fm_proj, grad_proj_z)
    ).astype(BF16)
    return (grad_embeds, (grad_fm_proj, grad_fm_mix, grad_fm_out, grad_lcb, grad_gain))


def run_layers(embeds, cot_rows, fm_proj, fm_mix, fm_out, lcb_weight, gain):
    depth = fm_proj.shape[0]
    inputs, saves = [], []
    current = embeds
    for layer in range(depth):
        inputs.append(current)
        current, saved = layer_forward(
            current, fm_proj[layer], fm_mix[layer], fm_out[layer], lcb_weight[layer], gain[layer]
        )
        saves.append(saved)
    back = cot_rows
    grad_list = [None] * depth
    for layer in reversed(range(depth)):
        back, grad_list[layer] = layer_backward(
            inputs[layer], back, saves[layer],
            fm_proj[layer], fm_mix[layer], fm_out[layer], lcb_weight[layer], gain[layer],
        )
    return current, back, grad_list


def pack(grads):
    proj, mix, out, lcb, gain = grads
    corner = jnp.pad(gain.reshape(3, 64), ((0, 29), (0, 0)))
    return jnp.concatenate([proj.T, mix, lcb, jnp.concatenate([out, corner], axis=1)], axis=0)


def shards(torus, pooled, owner_order, fm_proj, fm_mix, fm_out, lcb_weight, gain, cotangent):
    row_count = cotangent.shape[0]
    received = forward_exchange(torus, pooled)
    chosen = (owner_order[None, :] == jnp.arange(F, dtype=jnp.int32)[:, None]).astype(BF16)
    embeds = product("fs,nse->nfe", chosen, received.reshape(row_count, F, E)).astype(BF16)
    cot_rows = cotangent.reshape(row_count, F, E)
    result, grad_embeds, grad_list = run_layers(
        embeds, cot_rows, fm_proj, fm_mix, fm_out, lcb_weight, gain
    )
    layer_out = result.reshape(row_count, F * E)
    back_rows = product("fs,nfe->nse", chosen, grad_embeds).astype(BF16).reshape(row_count, F * E)
    packed = jnp.stack([pack(entry) for entry in grad_list]).astype(BF16)
    packed = jnp.pad(packed.reshape(2, 32, 10, 256), ((0, 0), (0, 0), (0, 6), (0, 0)))
    d_pooled, total = backward_exchange(torus, back_rows, packed.reshape(2, torus.y, torus.x, 16, 256))
    total = total.reshape(2, 32, 16, 256)[:, :, :10].reshape(2, 320, 256).astype(F32)
    total = total * (1.0 / pooled.shape[0])
    return (
        layer_out,
        d_pooled,
        total[:, :32].transpose(0, 2, 1),
        total[:, 32:160],
        total[:, 288:, :192],
        total[:, 160:288],
        total[:, 288:291, 192:].reshape(2, E),
    )


def solution(mesh):
    torus = Torus(6, mesh.shape["wide"] // 6, 2, mesh.shape["grp"] // 4)
    return jax.shard_map(
        functools.partial(shards, torus),
        mesh=mesh,
        in_specs=(P(None, ("wide", "grp")), P(), P(), P(), P(), P(), P(), P(("wide", "grp"), None)),
        out_specs=(P(("wide", "grp"), None), P(None, ("wide", "grp")), P(), P(), P(), P(), P()),
        check_vma=False,
    )
```

```python
import functools

import jax
import jax.numpy as jnp
from jax import lax
from jax.experimental import pallas as pl
from jax.experimental.pallas import tpu as pltpu
from jax.sharding import PartitionSpec as P

F = 256
E = 192
MESH = pl.DeviceIdType.MESH
BF16 = jnp.bfloat16
F32 = jnp.float32
DMA = pltpu.SemaphoreType.DMA


def wrap(value, size):
    return jnp.where(value >= size, value - size, value)


class Torus:
    def __init__(self, z_lo, y, z_hi, x):
        self.z_lo, self.y, self.z_hi, self.x = z_lo, y, z_hi, x
        self.z = z_lo * z_hi
        self.flat = y * x
        self.offsets = sorted(range(y), key=lambda o: -min(o, y - o))
        self.z_steps = sorted(range(1, self.z), key=lambda o: min(o, self.z - o))

    def place(self):
        wide, grp = lax.axis_index("wide"), lax.axis_index("grp")
        z_lo = lax.div(wide, self.y)
        z_hi = lax.div(grp, 2 * self.x)
        rest = grp - z_hi * 2 * self.x
        x = lax.div(rest, 2)
        return z_hi * self.z_lo + z_lo, wide - z_lo * self.y, x, rest - 2 * x

    def split(self, z):
        high = jnp.where(z >= self.z_lo, 1, 0)
        return z - high * self.z_lo, high

    def device(self, z, y, x, core):
        z_lo, z_hi = self.split(z)
        return (z_lo * self.y + y, z_hi * 2 * self.x + x * 2 + core)


def hello(torus):
    z, y, x, core = torus.place()
    barrier = pltpu.get_barrier_semaphore()

    def signal(where):
        pl.semaphore_signal(barrier, inc=1, device_id=where, device_id_type=MESH)

    signal(torus.device(z, y, x, 1 - core))
    for step in torus.z_steps:
        signal(torus.device(wrap(z + step, torus.z), y, x, core))
    for dy in torus.offsets:
        for dx in range(torus.x):
            if dy or dx:
                signal(torus.device(z, wrap(y + dy, torus.y), wrap(x + dx, torus.x), core))


def all_here(torus):
    pl.semaphore_wait(pltpu.get_barrier_semaphore(), torus.z + torus.flat - 1)


def remote(src, dst, send, recv, where):
    return pltpu.make_async_remote_copy(
        src_ref=src, dst_ref=dst, send_sem=send, recv_sem=recv, device_id=where, device_id_type=MESH
    )


def take(ref, sem):
    pltpu.make_async_copy(ref, ref, sem).wait()


def send_z(torus, i, src, middle, z_send, z_recv):
    z, y, x, core = torus.place()
    y_to = wrap(y + torus.offsets[i], torus.y)
    z_lo, z_hi = torus.split(z)
    landing = middle.at[z_lo, z_hi, y_to]
    pltpu.make_async_copy(src.at[z_lo, y_to, z_hi], landing, z_recv.at[i]).start()
    for step in torus.z_steps:
        z_to = wrap(z + step, torus.z)
        lo_to, hi_to = torus.split(z_to)
        block = src.at[lo_to, y_to, hi_to]
        remote(block, landing, z_send, z_recv.at[i], torus.device(z_to, y, x, core)).start()


def send_flat(torus, i, middle, out, f_send, f_recv, z_recv):
    z, y, x, core = torus.place()
    y_to = wrap(y + torus.offsets[i], torus.y)
    take(middle.at[:, :, y_to], z_recv.at[i])
    for dx in range(torus.x):
        x_to = wrap(x + dx, torus.x)
        block = middle.at[:, :, y_to, x_to]
        if torus.offsets[i] == 0 and dx == 0:
            pltpu.make_async_copy(block, out(y, x), f_recv.at[i]).start()
        else:
            remote(block, out(y, x), f_send, f_recv.at[i], torus.device(z, y_to, x_to, core)).start()


NT = (((1,), (1,)), ((), ()))
TN = (((0,), (0,)), ((), ()))
NN = (((1,), (0,)), ((), ()))
K = 32
HALF = 128
ROWS = 8
ACC = 2 * HALF + 2 * K


def dot(left, right, dims):
    return lax.dot_general(left, right, dims, preferred_element_type=F32)


def read_rows(tiles, b):
    first, middle, last = (tiles[pl.ds(8 * j + b, HALF, stride=24), :] for j in range(3))
    even = jnp.concatenate([first, middle[:, :64]], axis=1)
    odd = jnp.concatenate([middle[:, 64:], last], axis=1)
    return jnp.concatenate([even, odd], axis=0).astype(BF16)


def write_rows(tiles, b, rows):
    even, odd = rows[:HALF], rows[HALF:]
    parts = (even[:, :128], jnp.concatenate([even[:, 128:], odd[:, :64]], axis=1), odd[:, 64:])
    for j, part in enumerate(parts):
        tiles[pl.ds(8 * j + b, HALF, stride=24), :] = part


PLAN = [
    "z0", "z1", "z2", "a0", "a1", "z3", "a2", "z4", "z5", "z6", "z7", "y0", "y1", "f0", "y2", "y3", "f1", "a3",
    "y4", "f2", "a4", "y5", "f3", "y6", "f4", "a5", "y7", "f5", "f6", "f7",
]


def step_kernel(
    torus,
    p_ref, cot_ref, order_ref, proj_ref, mix_ref, out_ref, lcb_ref, gain_ref,
    y_ref, d_ref, t_ref,
    pieces, inbox, src, middle, landed, spare,
    tiles, chosen, chosen_t, spread, spread_t, front, front_t, x_in, normed, inv, z_t, m_t, q_t, gq_t, gi_t, stack,
    lcb_rows, fm_rows, cot_top, cot_mid, y_rows, acc,
    leaving, middle_b, pieces_b, y_tiles, g_ref, g_spare, g_inbox, g_half, x_parts, x_own, y_parts, y_own, z_parts,
    g_done, y_full, y_dense, x_full,
    c_send, c_recv, z_send, z_recv, f_send, f_recv,
    cb_send, cb_recv, zb_send, zb_recv, fb_send, fb_recv, g_send, g_recv,
):
    z, y, x, core = torus.place()
    mate = torus.device(z, y, x, 1 - core)
    run = torus.z_hi * torus.x * 16
    block_rows = torus.z_hi * torus.x * 8
    hello(torus)

    def prepare(i):
        y_to = wrap(y + torus.offsets[i], torus.y)

        def turn(z_lo, _):
            start = pl.multiple_of((z_lo * torus.y + y_to) * run, run)
            block = p_ref[:, pl.ds(start, run)].astype(F32)
            block = jnp.concatenate([block, block], axis=0).T.astype(BF16)
            pieces[z_lo, y_to] = block.reshape(torus.z_hi, torus.x, 2, 8, 128)
            return 0

        lax.fori_loop(0, torus.z_lo, turn, 0)

    swaps = []

    def swap(i):
        y_to = wrap(y + torus.offsets[i], torus.y)
        swaps.append(remote(
            pieces.at[:, y_to, :, :, 1 - core], inbox.at[:, y_to], c_send.at[i], c_recv.at[i], mate
        ))
        swaps[i].start()

    lanes = lax.broadcasted_iota(jnp.int32, (torus.x, 8, 128), 2)
    mine = jnp.where(lanes >= 64, 1, 0) == core

    def merge(i):
        y_to = wrap(y + torus.offsets[i], torus.y)
        swaps[i].wait_recv()

        def join(z_lo, _):
            for z_hi in range(torus.z_hi):
                own = pieces[z_lo, y_to, z_hi, :, core].astype(F32)
                other = inbox[z_lo, y_to, z_hi].astype(F32)
                src[z_lo, y_to, z_hi] = jnp.where(mine, own, other).astype(BF16)
            return 0

        lax.fori_loop(0, torus.z_lo, join, 0)
        send_z(torus, i, src, middle, z_send, z_recv)

    ahead = 2
    for i in range(ahead):
        prepare(i)
    all_here(torus)
    for i in range(ahead):
        swap(i)
    for i in range(torus.y):
        if i + ahead < torus.y:
            prepare(i + ahead)
            swap(i + ahead)
        merge(i)

    spots = lax.broadcasted_iota(jnp.int32, (F, F), 0)
    places = lax.broadcasted_iota(jnp.int32, (F, F), 1)
    apart = (spots == jnp.where(places >= HALF, 2 * places - F + 1, 2 * places)).astype(F32)
    spread[...] = apart.astype(BF16)
    spread_t[...] = apart.T.astype(BF16)
    match = dot((spots == order_ref[...]).astype(BF16), spread[...], NN)
    chosen[...] = match.astype(BF16)
    chosen_t[...] = match.T.astype(BF16)
    for l in range(2):
        front[l, :HALF] = lcb_ref[l]
        front[l, HALF:] = proj_ref[l]
        front_t[l, :, :HALF] = lcb_ref[l].astype(F32).T.astype(BF16)
        front_t[l, :, HALF:] = proj_ref[l].astype(F32).T.astype(BF16)

    def open_cot(k, _):
        rows = cot_ref[pl.ds(8 * k, 8)].astype(F32).reshape(64, 128)
        tiles[pl.ds(pl.multiple_of(64 * k, 64), 64), :] = rows
        return 0

    lax.fori_loop(0, torus.z * torus.flat // 8, open_cot, 0)
    for i in range(torus.y):
        send_flat(torus, i, middle, lambda y, x: landed.at[:, y, :, x], f_send, f_recv, z_recv)
        cot_top[i] = dot(spread[...], read_rows(tiles, i), NN).astype(BF16)
    for i in range(torus.y):
        y_from = wrap(y - torus.offsets[i] + torus.y, torus.y)
        take(landed.at[:, y_from], f_recv.at[i])

        def open_rows(z_lo, _):
            start = pl.multiple_of((z_lo * torus.y + y_from) * block_rows, block_rows)
            tiles[pl.ds(start, block_rows), :] = landed[z_lo, y_from].astype(F32).reshape(block_rows, 128)
            return 0

        lax.fori_loop(0, torus.z_lo, open_rows, 0)

    for b in range(ROWS):
        x_in[0, b] = dot(chosen[...], read_rows(tiles, b), NN).astype(BF16)
    for l in range(2):
        for b in range(ROWS):
            mixed = dot(front[l], x_in[l, b], NN)
            lcb_rows[b] = mixed[:HALF]
            z_t[l, b] = mixed[HALF:].astype(BF16)
        for b in range(ROWS):
            m_t[l, K * b : K * (b + 1)] = dot(z_t[l, b], x_in[l, b], NT).astype(BF16)
        q_t[l] = dot(m_t[l], mix_ref[l], NT).astype(BF16)
        for b in range(ROWS):
            for half in range(2):
                rows = slice(half * HALF, (half + 1) * HALF)
                branch = lcb_rows[b] if half else dot(q_t[l, K * b : K * (b + 1)], out_ref[l], TN)
                summed = branch + x_in[l, b, rows].astype(F32)
                center = summed - jnp.sum(summed, axis=-1, keepdims=True) * (1.0 / E)
                variance = jnp.sum(center * center, axis=-1, keepdims=True) * (1.0 / E)
                scale = lax.rsqrt(variance + 1e-05)
                inv[l, b, rows] = scale
                value = center * scale
                normed[l, b, rows] = value
                result = (value * gain_ref[l]).astype(BF16)
                if l == 0:
                    x_in[1, b, rows] = result
                else:
                    y_rows[b, rows] = result

    pair = remote(g_ref.at[1 - core], g_inbox, g_send.at[0], g_recv.at[0], mate)
    share = g_ref.shape[2] // torus.y
    for l in (1, 0):
        gain_total = jnp.zeros((8, E), F32)
        for b in range(ROWS):
            for half in range(2):
                rows = slice(half * HALF, (half + 1) * HALF)
                cot = (cot_top if l else cot_mid)[b, rows].astype(F32)
                value = normed[l, b, rows]
                gain_total += jnp.sum((cot * value).reshape(HALF // 8, 8, E), axis=0)
                d_norm = cot * gain_ref[l]
                mean = jnp.sum(d_norm, axis=-1, keepdims=True) * (1.0 / E)
                along = jnp.sum(d_norm * value, axis=-1, keepdims=True) * (1.0 / E)
                grad = (inv[l, b, rows] * (d_norm - mean - value * along)).astype(BF16)
                if half:
                    stack[b, :HALF] = grad
                else:
                    fm_rows[b] = grad
        for b in range(ROWS):
            gq_t[K * b : K * (b + 1)] = dot(out_ref[l], fm_rows[b], NT).astype(BF16)
        gi_t[...] = dot(gq_t[...], mix_ref[l], NN).astype(BF16)
        acc[:HALF] = dot(gq_t[...], m_t[l], TN)
        out_total = jnp.zeros((K, E), F32)
        for b in range(ROWS):
            out_total += dot(q_t[l, K * b : K * (b + 1)], fm_rows[b], NN)
            stack[b, HALF:] = dot(gi_t[K * b : K * (b + 1)], x_in[l, b], NN).astype(BF16)
        front_total = jnp.zeros((HALF + K, F), F32)
        for b in range(ROWS):
            front_total += dot(stack[b], x_in[l, b], NT)
        acc[2 * HALF : 2 * HALF + K] = front_total[HALF:]
        acc[HALF : 2 * HALF] = front_total[:HALF]
        gain_row = jnp.sum(gain_total, axis=0, keepdims=True)
        acc[K + 2 * HALF :, :E] = out_total
        acc[K + 2 * HALF :, E:] = jnp.zeros((K, F - E), F32)
        for part in range(3):
            acc[K + 2 * HALF + part : K + 2 * HALF + part + 1, E:] = gain_row[:, part * 64 : (part + 1) * 64]
        for k in range(torus.x):
            depth = torus.y * share
            g_ref[l, k] = acc[k * depth : (k + 1) * depth].astype(BF16)
        if l == 0:
            pair.start()
        for b in range(ROWS):
            total = dot(front_t[l], stack[b], NN) + dot(gi_t[K * b : K * (b + 1)], z_t[l, b], TN)
            total += jnp.concatenate([fm_rows[b], stack[b, :HALF]], axis=0).astype(F32)
            total = total.astype(BF16)
            if l:
                cot_mid[b] = total
            else:
                write_rows(tiles, b, dot(chosen_t[...], total, NN))

    def leave(i):
        y_to = wrap(y + torus.offsets[i], torus.y)

        def close(z_lo, _):
            start = pl.multiple_of((z_lo * torus.y + y_to) * block_rows, block_rows)
            rows = tiles[pl.ds(start, block_rows), :].reshape(torus.z_hi, torus.x, 8, 128)
            leaving[z_lo, y_to] = rows.astype(BF16)
            return 0

        lax.fori_loop(0, torus.z_lo, close, 0)
        send_z(torus, i, leaving, middle_b, zb_send, zb_recv)

    def along_x(block, landing, k):
        pltpu.make_async_copy(block(x), landing, g_recv.at[k]).start()
        for dx in range(1, torus.x):
            x_to = wrap(x + dx, torus.x)
            remote(block(x_to), landing, g_send.at[k], g_recv.at[k], torus.device(z, y, x_to, core)).start()

    def along_y(block, landing, k):
        pltpu.make_async_copy(block(y), landing, g_recv.at[k]).start()
        for dy in range(1, torus.y):
            y_to = wrap(y + dy, torus.y)
            remote(block(y_to), landing, g_send.at[k], g_recv.at[k], torus.device(z, y_to, x, core)).start()

    def sum_pair():
        pair.wait_recv()

        def add(k, _):
            g_half[k] = (g_ref[core, k].astype(F32) + g_inbox[k].astype(F32)).astype(BF16)
            return 0

        lax.fori_loop(0, torus.x, add, 0)
        along_x(lambda x_to: g_half.at[x_to], x_parts.at[x], 1)

    def sum_x():
        take(x_parts, g_recv.at[1])
        total = jnp.sum(x_parts[...].astype(F32), axis=0)
        rest = jnp.zeros((16 - share, F), F32)
        for k in range(torus.y):
            x_own[k] = jnp.concatenate([total[k * share : (k + 1) * share], rest], axis=0).astype(BF16)
        along_y(lambda y_to: x_own.at[y_to], y_parts.at[y], 2)

    def sum_y():
        take(y_parts, g_recv.at[2])
        y_own[...] = jnp.sum(y_parts[...].astype(F32), axis=0).astype(BF16)
        landing = z_parts.at[z]
        pltpu.make_async_copy(y_own, landing, g_recv.at[3]).start()
        for step in torus.z_steps:
            where = torus.device(wrap(z + step, torus.z), y, x, core)
            remote(y_own, landing, g_send.at[3], g_recv.at[3], where).start()

    def sum_z():
        take(z_parts, g_recv.at[3])
        g_done[...] = jnp.sum(z_parts[...].astype(F32), axis=0).astype(BF16)
        along_y(lambda y_to: g_done, y_full.at[y], 4)

    def share_x():
        take(y_full, g_recv.at[4])
        y_dense[...] = jnp.concatenate(
            [y_full[k].astype(F32)[:share] for k in range(torus.y)], axis=0
        ).astype(BF16)
        along_x(lambda x_to: y_dense, x_full.at[x], 5)

    last = remote(x_full, t_ref.at[core], g_send.at[6], g_recv.at[6], mate)

    def share_pair():
        take(x_full, g_recv.at[5])
        last.start()
        t_ref[core] = x_full[...]

    parts = [sum_pair, sum_x, sum_y, sum_z, share_x, share_pair]
    for step in PLAN:
        kind, i = step[0], int(step[1:])
        if kind == "a":
            parts[i]()
        elif kind == "z":
            leave(i)
        elif kind == "y":
            write_rows(y_tiles, i, dot(spread_t[...], y_rows[i], NN))
        else:
            send_flat(torus, i, middle_b, lambda y, x: pieces_b.at[:, y, :, x, core], fb_send, fb_recv, zb_recv)

    def close_y(k, _):
        rows = y_tiles[pl.ds(pl.multiple_of(64 * k, 64), 64), :].reshape(8, 8, 128)
        y_ref[pl.ds(8 * k, 8)] = rows.astype(BF16)
        return 0

    lax.fori_loop(0, torus.z * torus.flat // 8, close_y, 0)
    swaps_b = []

    def swap_b(i):
        y_from = wrap(y - torus.offsets[i] + torus.y, torus.y)
        block = pieces_b.at[:, y_from, :, :, core]
        take(block, fb_recv.at[i])
        swaps_b.append(remote(block, block, cb_send.at[i], cb_recv.at[i], mate))
        swaps_b[i].start()

    def finish(i):
        y_from = wrap(y - torus.offsets[i] + torus.y, torus.y)
        swaps_b[i].wait_recv()

        def turn(z_lo, _):
            start = pl.multiple_of((z_lo * torus.y + y_from) * run, run)
            block = pieces_b[z_lo, y_from].astype(F32).reshape(run, 128).T
            d_ref[:, pl.ds(start, run)] = jnp.where(core == 0, block[:64], block[64:]).astype(BF16)
            return 0

        lax.fori_loop(0, torus.z_lo, turn, 0)

    for i in range(torus.y):
        swap_b(i)
        if i:
            finish(i - 1)
    finish(torus.y - 1)
    last.wait()
    for i in range(torus.y):
        swaps[i].wait_send()
        swaps_b[i].wait_send()
    pair.wait_send()
    for sem in (z_send, zb_send):
        take(spare.at[pl.ds(0, (torus.z - 1) * torus.y * torus.x)], sem)
    for sem in (f_send, fb_send):
        take(spare.at[pl.ds(0, (torus.flat - 1) * torus.z)], sem)
    take(x_parts.at[pl.ds(0, torus.x - 1)], g_send.at[1])
    take(g_spare.at[pl.ds(0, torus.y - 1)], g_send.at[2])
    take(g_spare.at[pl.ds(0, torus.z - 1)], g_send.at[3])
    take(g_spare.at[pl.ds(0, torus.y - 1)], g_send.at[4])
    take(x_full.at[pl.ds(0, torus.x - 1)], g_send.at[5])


def shards(torus, pooled, owner_order, fm_proj, fm_mix, fm_out, lcb_weight, gain, cotangent):
    chips = torus.z * torus.flat
    shape = (torus.z_lo, torus.y, torus.z_hi, torus.x, 8, 128)
    both = shape[:4] + (2, 8, 128)
    middle = (torus.z_lo, torus.z_hi, torus.y, torus.x, 8, 128)
    whole = (ROWS, F, E)
    depth = ACC // torus.x
    half = (torus.x, depth, F)
    chunk = (16, F)
    vmem = pl.BlockSpec(memory_space=pltpu.VMEM)
    spare = max((torus.z - 1) * torus.y * torus.x, (torus.flat - 1) * torus.z)
    y_tiles, d_turned, total = pl.pallas_call(
        functools.partial(step_kernel, torus),
        out_shape=(
            jax.ShapeDtypeStruct((chips, 8, 128), BF16),
            jax.ShapeDtypeStruct((64, chips * 16), BF16),
            jax.ShapeDtypeStruct((2,) + half, BF16),
        ),
        in_specs=[vmem] * 8,
        out_specs=[vmem] * 3,
        scratch_shapes=[
            pltpu.VMEM(both, BF16),
            pltpu.VMEM(shape, BF16),
            pltpu.VMEM(shape, BF16),
            pltpu.VMEM(middle, BF16),
            pltpu.VMEM(shape, BF16),
            pltpu.VMEM((spare, 8, 128), BF16),
            pltpu.VMEM((chips * 8, 128), F32),
            pltpu.VMEM((F, F), BF16),
            pltpu.VMEM((F, F), BF16),
            pltpu.VMEM((F, F), BF16),
            pltpu.VMEM((F, F), BF16),
            pltpu.VMEM((2, HALF + K, F), BF16),
            pltpu.VMEM((2, F, HALF + K), BF16),
            pltpu.VMEM((2,) + whole, BF16),
            pltpu.VMEM((2,) + whole, F32),
            pltpu.VMEM((2, ROWS, F, 1), F32),
            pltpu.VMEM((2, ROWS, K, E), BF16),
            pltpu.VMEM((2, ROWS * K, F), BF16),
            pltpu.VMEM((2, ROWS * K, HALF), BF16),
            pltpu.VMEM((ROWS * K, HALF), BF16),
            pltpu.VMEM((ROWS * K, F), BF16),
            pltpu.VMEM((ROWS, HALF + K, E), BF16),
            pltpu.VMEM((ROWS, HALF, E), F32),
            pltpu.VMEM((ROWS, HALF, E), BF16),
            pltpu.VMEM(whole, BF16),
            pltpu.VMEM(whole, BF16),
            pltpu.VMEM(whole, BF16),
            pltpu.VMEM((ACC, F), F32),
            pltpu.VMEM(shape, BF16),
            pltpu.VMEM(middle, BF16),
            pltpu.VMEM(both, BF16),
            pltpu.VMEM((chips * 8, 128), F32),
            pltpu.VMEM((2,) + half, BF16),
            pltpu.VMEM((max(torus.y, torus.z) - 1,) + chunk, BF16),
            pltpu.VMEM(half, BF16),
            pltpu.VMEM(half, BF16),
            pltpu.VMEM(half, BF16),
            pltpu.VMEM((torus.y,) + chunk, BF16),
            pltpu.VMEM((torus.y,) + chunk, BF16),
            pltpu.VMEM(chunk, BF16),
            pltpu.VMEM((torus.z,) + chunk, BF16),
            pltpu.VMEM(chunk, BF16),
            pltpu.VMEM((torus.y,) + chunk, BF16),
            pltpu.VMEM(half[1:], BF16),
            pltpu.VMEM(half, BF16),
        ]
        + [DMA((torus.y,)), DMA((torus.y,)), DMA, DMA((torus.y,)), DMA, DMA((torus.y,))] * 2
        + [DMA((7,)), DMA((7,))],
        compiler_params=pltpu.CompilerParams(
            collective_id=0, has_side_effects=True, vmem_limit_bytes=56 * 1024 * 1024
        ),
        name="train_step",
    )(
        pooled.T, cotangent.reshape(ROWS, chips, 128).transpose(1, 0, 2), owner_order.reshape(1, F),
        fm_proj.transpose(0, 2, 1), fm_mix, fm_out, lcb_weight, gain.reshape(2, 1, E),
    )
    total = total.reshape(2, -1, F).astype(F32) * (1.0 / pooled.shape[0])
    return (
        y_tiles.transpose(1, 0, 2).reshape(ROWS, F * E),
        d_turned.T,
        total[:, F : F + K].transpose(0, 2, 1),
        total[:, :HALF],
        total[:, F + K :, :E],
        total[:, HALF:F],
        total[:, F + K : F + K + 3, E:].reshape(2, E),
    )


def solution(mesh):
    torus = Torus(6, mesh.shape["wide"] // 6, 2, mesh.shape["grp"] // 4)
    return jax.shard_map(
        functools.partial(shards, torus),
        mesh=mesh,
        in_specs=(P(None, ("wide", "grp")), P(), P(), P(), P(), P(), P(), P(("wide", "grp"), None)),
        out_specs=(P(("wide", "grp"), None), P(None, ("wide", "grp")), P(), P(), P(), P(), P()),
        check_vma=False,
    )
```

```python
import functools

import jax
import jax.numpy as jnp
from jax import lax
from jax.experimental import pallas as pl
from jax.experimental.pallas import tpu as pltpu
from jax.sharding import PartitionSpec as P

F = 256
E = 192
MESH = pl.DeviceIdType.MESH
BF16 = jnp.bfloat16
F32 = jnp.float32
DMA = pltpu.SemaphoreType.DMA


def wrap(value, size):
    return jnp.where(value >= size, value - size, value)


class Torus:
    def __init__(self, z_lo, y, z_hi, x):
        self.z_lo, self.y, self.z_hi, self.x = z_lo, y, z_hi, x
        self.z = z_lo * z_hi
        self.flat = y * x
        self.offsets = sorted(range(y), key=lambda o: -min(o, y - o))
        self.z_steps = sorted(range(1, self.z), key=lambda o: min(o, self.z - o))

    def place(self):
        wide, grp = lax.axis_index("wide"), lax.axis_index("grp")
        z_lo = lax.div(wide, self.y)
        z_hi = lax.div(grp, 2 * self.x)
        rest = grp - z_hi * 2 * self.x
        x = lax.div(rest, 2)
        return z_hi * self.z_lo + z_lo, wide - z_lo * self.y, x, rest - 2 * x

    def split(self, z):
        high = jnp.where(z >= self.z_lo, 1, 0)
        return z - high * self.z_lo, high

    def device(self, z, y, x, core):
        z_lo, z_hi = self.split(z)
        return (z_lo * self.y + y, z_hi * 2 * self.x + x * 2 + core)


def hello(torus):
    z, y, x, core = torus.place()
    barrier = pltpu.get_barrier_semaphore()

    def signal(where):
        pl.semaphore_signal(barrier, inc=1, device_id=where, device_id_type=MESH)

    signal(torus.device(z, y, x, 1 - core))
    for step in torus.z_steps:
        signal(torus.device(wrap(z + step, torus.z), y, x, core))
    for dy in torus.offsets:
        for dx in range(torus.x):
            if dy or dx:
                signal(torus.device(z, wrap(y + dy, torus.y), wrap(x + dx, torus.x), core))


def all_here(torus):
    pl.semaphore_wait(pltpu.get_barrier_semaphore(), torus.z + torus.flat - 1)


def remote(src, dst, send, recv, where):
    return pltpu.make_async_remote_copy(
        src_ref=src, dst_ref=dst, send_sem=send, recv_sem=recv, device_id=where, device_id_type=MESH
    )


def take(ref, sem):
    pltpu.make_async_copy(ref, ref, sem).wait()


def send_z(torus, i, src, middle, z_send, z_recv):
    z, y, x, core = torus.place()
    y_to = wrap(y + torus.offsets[i], torus.y)
    z_lo, z_hi = torus.split(z)
    landing = middle.at[z_lo, z_hi, y_to]
    pltpu.make_async_copy(src.at[z_lo, y_to, z_hi], landing, z_recv.at[i]).start()
    for step in torus.z_steps:
        z_to = wrap(z + step, torus.z)
        lo_to, hi_to = torus.split(z_to)
        block = src.at[lo_to, y_to, hi_to]
        remote(block, landing, z_send, z_recv.at[i], torus.device(z_to, y, x, core)).start()


def send_flat(torus, i, middle, out, f_send, f_recv, z_recv):
    z, y, x, core = torus.place()
    y_to = wrap(y + torus.offsets[i], torus.y)
    take(middle.at[:, :, y_to], z_recv.at[i])
    for dx in range(torus.x):
        x_to = wrap(x + dx, torus.x)
        block = middle.at[:, :, y_to, x_to]
        if torus.offsets[i] == 0 and dx == 0:
            pltpu.make_async_copy(block, out(y, x), f_recv.at[i]).start()
        else:
            remote(block, out(y, x), f_send, f_recv.at[i], torus.device(z, y_to, x_to, core)).start()


NT = (((1,), (1,)), ((), ()))
TN = (((0,), (0,)), ((), ()))
NN = (((1,), (0,)), ((), ()))
K = 32
HALF = 128
ROWS = 8
ACC = 2 * HALF + 2 * K


def dot(left, right, dims):
    return lax.dot_general(left, right, dims, preferred_element_type=F32)


def read_rows(tiles, b):
    first, middle, last = (tiles[pl.ds(8 * j + b, HALF, stride=24), :] for j in range(3))
    even = jnp.concatenate([first, middle[:, :64]], axis=1)
    odd = jnp.concatenate([middle[:, 64:], last], axis=1)
    return jnp.concatenate([even, odd], axis=0).astype(BF16)


def write_rows(tiles, b, rows):
    even, odd = rows[:HALF], rows[HALF:]
    parts = (even[:, :128], jnp.concatenate([even[:, 128:], odd[:, :64]], axis=1), odd[:, 64:])
    for j, part in enumerate(parts):
        tiles[pl.ds(8 * j + b, HALF, stride=24), :] = part


PLAN = [
    "z0", "z1", "z2", "a0", "a1", "a2", "z3", "z4", "z5", "z6", "z7", "f0", "f1", "f2", "y0", "y1", "a3", "y2", "y3",
    "f3", "y4", "a4", "y5", "f4", "f5", "a5", "y6", "f6", "y7", "f7",
]


def step_kernel(
    torus,
    p_far, cot_far, order_far, proj_far, mix_far, out_far, lcb_far, gain_far,
    y_ref, d_ref, proj_sum, mix_sum, out_sum, lcb_sum, gain_sum,
    p_ref, cot_ref, order_ref, proj_ref, mix_ref, out_ref, lcb_ref, gain_ref, t_ref,
    pieces, inbox, src, middle, landed, spare,
    tiles, chosen, chosen_t, spread, spread_t, front, front_t, x_in, normed, inv, z_t, m_t, q_t, gq_t, gi_t, stack,
    lcb_rows, fm_rows, cot_top, cot_mid, y_rows, acc,
    leaving, middle_b, pieces_b, y_tiles, g_ref, g_spare, g_inbox, g_half, x_parts, x_own, y_parts, y_own, z_parts,
    g_done, y_full, y_dense, x_full,
    c_send, c_recv, z_send, z_recv, f_send, f_recv,
    cb_send, cb_recv, zb_send, zb_recv, fb_send, fb_recv, g_send, g_recv, near,
):
    z, y, x, core = torus.place()
    mate = torus.device(z, y, x, 1 - core)
    run = torus.z_hi * torus.x * 16
    block_rows = torus.z_hi * torus.x * 8
    far = (p_far, cot_far, order_far, proj_far, mix_far, out_far, lcb_far, gain_far)
    here = (p_ref, cot_ref, order_ref, proj_ref, mix_ref, out_ref, lcb_ref, gain_ref)
    loads = [pltpu.make_async_copy(a, b, near.at[k]) for k, (a, b) in enumerate(zip(far, here))]
    for load in loads:
        load.start()
    hello(torus)

    def prepare(i):
        y_to = wrap(y + torus.offsets[i], torus.y)

        def turn(z_lo, _):
            start = pl.multiple_of((z_lo * torus.y + y_to) * run, run)
            block = p_ref[:, pl.ds(start, run)].astype(F32)
            block = jnp.concatenate([block, block], axis=0).T.astype(BF16)
            pieces[z_lo, y_to] = block.reshape(torus.z_hi, torus.x, 2, 8, 128)
            return 0

        lax.fori_loop(0, torus.z_lo, turn, 0)

    swaps = []

    def swap(i):
        y_to = wrap(y + torus.offsets[i], torus.y)
        swaps.append(remote(
            pieces.at[:, y_to, :, :, 1 - core], inbox.at[:, y_to], c_send.at[i], c_recv.at[i], mate
        ))
        swaps[i].start()

    lanes = lax.broadcasted_iota(jnp.int32, (torus.x, 8, 128), 2)
    mine = jnp.where(lanes >= 64, 1, 0) == core

    def merge(i):
        y_to = wrap(y + torus.offsets[i], torus.y)
        swaps[i].wait_recv()

        def join(z_lo, _):
            for z_hi in range(torus.z_hi):
                own = pieces[z_lo, y_to, z_hi, :, core].astype(F32)
                other = inbox[z_lo, y_to, z_hi].astype(F32)
                src[z_lo, y_to, z_hi] = jnp.where(mine, own, other).astype(BF16)
            return 0

        lax.fori_loop(0, torus.z_lo, join, 0)
        send_z(torus, i, src, middle, z_send, z_recv)

    loads[0].wait()
    prepare(0)
    all_here(torus)
    swap(0)
    prepare(1)
    swap(1)
    for i in range(torus.y):
        merge(i)
        if i + 2 < torus.y:
            prepare(i + 2)
            swap(i + 2)

    for load in loads[1:]:
        load.wait()
    spots = lax.broadcasted_iota(jnp.int32, (F, F), 0)
    places = lax.broadcasted_iota(jnp.int32, (F, F), 1)
    apart = (spots == jnp.where(places >= HALF, 2 * places - F + 1, 2 * places)).astype(F32)
    spread[...] = apart.astype(BF16)
    spread_t[...] = apart.T.astype(BF16)
    match = dot((spots == order_ref[...]).astype(BF16), spread[...], NN)
    chosen[...] = match.astype(BF16)
    chosen_t[...] = match.T.astype(BF16)
    for l in range(2):
        front[l, :HALF] = lcb_ref[l]
        front[l, HALF:] = proj_ref[l]
        front_t[l, :, :HALF] = lcb_ref[l].astype(F32).T.astype(BF16)
        front_t[l, :, HALF:] = proj_ref[l].astype(F32).T.astype(BF16)

    def open_cot(k, _):
        rows = cot_ref[pl.ds(8 * k, 8)].astype(F32).reshape(64, 128)
        tiles[pl.ds(pl.multiple_of(64 * k, 64), 64), :] = rows
        return 0

    lax.fori_loop(0, torus.z * torus.flat // 8, open_cot, 0)
    for i in range(torus.y):
        send_flat(torus, i, middle, lambda y, x: landed.at[:, y, :, x], f_send, f_recv, z_recv)
        cot_top[i] = dot(spread[...], read_rows(tiles, i), NN).astype(BF16)
    for i in range(torus.y):
        y_from = wrap(y - torus.offsets[i] + torus.y, torus.y)
        take(landed.at[:, y_from], f_recv.at[i])

        def open_rows(z_lo, _):
            start = pl.multiple_of((z_lo * torus.y + y_from) * block_rows, block_rows)
            tiles[pl.ds(start, block_rows), :] = landed[z_lo, y_from].astype(F32).reshape(block_rows, 128)
            return 0

        lax.fori_loop(0, torus.z_lo, open_rows, 0)

    for b in range(ROWS):
        x_in[0, b] = dot(chosen[...], read_rows(tiles, b), NN).astype(BF16)
    for l in range(2):
        for b in range(ROWS):
            mixed = dot(front[l], x_in[l, b], NN)
            lcb_rows[b] = mixed[:HALF]
            z_t[l, b] = mixed[HALF:].astype(BF16)
        for b in range(ROWS):
            m_t[l, K * b : K * (b + 1)] = dot(z_t[l, b], x_in[l, b], NT).astype(BF16)
        q_t[l] = dot(m_t[l], mix_ref[l], NT).astype(BF16)
        for b in range(ROWS):
            for half in range(2):
                rows = slice(half * HALF, (half + 1) * HALF)
                branch = lcb_rows[b] if half else dot(q_t[l, K * b : K * (b + 1)], out_ref[l], TN)
                summed = branch + x_in[l, b, rows].astype(F32)
                center = summed - jnp.sum(summed, axis=-1, keepdims=True) * (1.0 / E)
                variance = jnp.sum(center * center, axis=-1, keepdims=True) * (1.0 / E)
                scale = lax.rsqrt(variance + 1e-05)
                inv[l, b, rows] = scale
                value = center * scale
                normed[l, b, rows] = value
                result = (value * gain_ref[l : l + 1]).astype(BF16)
                if l == 0:
                    x_in[1, b, rows] = result
                else:
                    y_rows[b, rows] = result

    pair = remote(g_ref.at[1 - core], g_inbox, g_send.at[0], g_recv.at[0], mate)
    share = g_ref.shape[2] // torus.y
    for l in (1, 0):
        gain_total = jnp.zeros((8, E), F32)
        for b in range(ROWS):
            for half in range(2):
                rows = slice(half * HALF, (half + 1) * HALF)
                cot = (cot_top if l else cot_mid)[b, rows].astype(F32)
                value = normed[l, b, rows]
                gain_total += jnp.sum((cot * value).reshape(HALF // 8, 8, E), axis=0)
                d_norm = cot * gain_ref[l : l + 1]
                mean = jnp.sum(d_norm, axis=-1, keepdims=True) * (1.0 / E)
                along = jnp.sum(d_norm * value, axis=-1, keepdims=True) * (1.0 / E)
                grad = (inv[l, b, rows] * (d_norm - mean - value * along)).astype(BF16)
                if half:
                    stack[b, :HALF] = grad
                else:
                    fm_rows[b] = grad
        for b in range(ROWS):
            gq_t[K * b : K * (b + 1)] = dot(out_ref[l], fm_rows[b], NT).astype(BF16)
        gi_t[...] = dot(gq_t[...], mix_ref[l], NN).astype(BF16)
        acc[:HALF] = dot(gq_t[...], m_t[l], TN)
        out_total = jnp.zeros((K, E), F32)
        for b in range(ROWS):
            out_total += dot(q_t[l, K * b : K * (b + 1)], fm_rows[b], NN)
            stack[b, HALF:] = dot(gi_t[K * b : K * (b + 1)], x_in[l, b], NN).astype(BF16)
        front_total = jnp.zeros((HALF + K, F), F32)
        for b in range(ROWS):
            front_total += dot(stack[b], x_in[l, b], NT)
        acc[2 * HALF : 2 * HALF + K] = front_total[HALF:]
        acc[HALF : 2 * HALF] = front_total[:HALF]
        gain_row = jnp.sum(gain_total, axis=0, keepdims=True)
        acc[K + 2 * HALF :, :E] = out_total
        acc[K + 2 * HALF :, E:] = jnp.zeros((K, F - E), F32)
        for part in range(3):
            acc[K + 2 * HALF + part : K + 2 * HALF + part + 1, E:] = gain_row[:, part * 64 : (part + 1) * 64]
        for k in range(torus.x):
            depth = torus.y * share
            g_ref[l, k] = acc[k * depth : (k + 1) * depth].astype(BF16)
        if l == 0:
            pair.start()
        for b in range(ROWS):
            total = dot(front_t[l], stack[b], NN) + dot(gi_t[K * b : K * (b + 1)], z_t[l, b], TN)
            total += jnp.concatenate([fm_rows[b], stack[b, :HALF]], axis=0).astype(F32)
            cot_mid[b] = total.astype(BF16)
    for b in range(ROWS):
        write_rows(tiles, b, dot(chosen_t[...], cot_mid[b], NN))

    def leave(i):
        y_to = wrap(y + torus.offsets[i], torus.y)

        def close(z_lo, _):
            start = pl.multiple_of((z_lo * torus.y + y_to) * block_rows, block_rows)
            rows = tiles[pl.ds(start, block_rows), :].reshape(torus.z_hi, torus.x, 8, 128)
            leaving[z_lo, y_to] = rows.astype(BF16)
            return 0

        lax.fori_loop(0, torus.z_lo, close, 0)
        send_z(torus, i, leaving, middle_b, zb_send, zb_recv)

    def along_x(block, landing, k):
        pltpu.make_async_copy(block(x), landing, g_recv.at[k]).start()
        for dx in range(1, torus.x):
            x_to = wrap(x + dx, torus.x)
            remote(block(x_to), landing, g_send.at[k], g_recv.at[k], torus.device(z, y, x_to, core)).start()

    def along_y(block, landing, k):
        pltpu.make_async_copy(block(y), landing, g_recv.at[k]).start()
        for dy in range(1, torus.y):
            y_to = wrap(y + dy, torus.y)
            remote(block(y_to), landing, g_send.at[k], g_recv.at[k], torus.device(z, y_to, x, core)).start()

    def sum_pair():
        pair.wait_recv()

        def add(k, _):
            g_half[k] = (g_ref[core, k].astype(F32) + g_inbox[k].astype(F32)).astype(BF16)
            return 0

        lax.fori_loop(0, torus.x, add, 0)
        along_x(lambda x_to: g_half.at[x_to], x_parts.at[x], 1)

    def sum_x():
        take(x_parts, g_recv.at[1])
        total = jnp.sum(x_parts[...].astype(F32), axis=0)
        rest = jnp.zeros((16 - share, F), F32)
        for k in range(torus.y):
            x_own[k] = jnp.concatenate([total[k * share : (k + 1) * share], rest], axis=0).astype(BF16)
        along_y(lambda y_to: x_own.at[y_to], y_parts.at[y], 2)

    def sum_y():
        take(y_parts, g_recv.at[2])
        y_own[...] = jnp.sum(y_parts[...].astype(F32), axis=0).astype(BF16)
        landing = z_parts.at[z]
        pltpu.make_async_copy(y_own, landing, g_recv.at[3]).start()
        for step in torus.z_steps:
            where = torus.device(wrap(z + step, torus.z), y, x, core)
            remote(y_own, landing, g_send.at[3], g_recv.at[3], where).start()

    def sum_z():
        take(z_parts, g_recv.at[3])
        g_done[...] = jnp.sum(z_parts[...].astype(F32), axis=0).astype(BF16)
        along_y(lambda y_to: g_done, y_full.at[y], 4)

    def share_x():
        take(y_full, g_recv.at[4])
        y_dense[...] = jnp.concatenate(
            [y_full[k].astype(F32)[:share] for k in range(torus.y)], axis=0
        ).astype(BF16)
        along_x(lambda x_to: y_dense, x_full.at[x], 5)

    last = remote(x_full, t_ref.at[core], g_send.at[6], g_recv.at[6], mate)

    def share_pair():
        take(x_full, g_recv.at[5])
        last.start()
        t_ref[core] = x_full[...]

    parts = [sum_pair, sum_x, sum_y, sum_z, share_x, share_pair]
    for step in PLAN:
        kind, i = step[0], int(step[1:])
        if kind == "a":
            parts[i]()
        elif kind == "z":
            leave(i)
        elif kind == "y":
            write_rows(y_tiles, i, dot(spread_t[...], y_rows[i], NN))
        else:
            send_flat(torus, i, middle_b, lambda y, x: pieces_b.at[:, y, :, x, core], fb_send, fb_recv, zb_recv)

    def close_y(k, _):
        rows = y_tiles[pl.ds(pl.multiple_of(64 * k, 64), 64), :].reshape(8, 8, 128)
        y_ref[pl.ds(8 * k, 8)] = rows.astype(BF16)
        return 0

    lax.fori_loop(0, torus.z * torus.flat // 8, close_y, 0)
    swaps_b = []

    def swap_b(i):
        y_from = wrap(y - torus.offsets[i] + torus.y, torus.y)
        block = pieces_b.at[:, y_from, :, :, core]
        take(block, fb_recv.at[i])
        swaps_b.append(remote(block, block, cb_send.at[i], cb_recv.at[i], mate))
        swaps_b[i].start()

    def finish(i):
        y_from = wrap(y - torus.offsets[i] + torus.y, torus.y)
        swaps_b[i].wait_recv()

        def turn(z_lo, _):
            start = pl.multiple_of((z_lo * torus.y + y_from) * run, run)
            block = pieces_b[z_lo, y_from].astype(F32).reshape(run, 128).T
            d_ref[:, pl.ds(start, run)] = jnp.where(core == 0, block[:64], block[64:]).astype(BF16)
            return 0

        lax.fori_loop(0, torus.z_lo, turn, 0)

    for i in range(torus.y - 1):
        swap_b(i)
        if i:
            finish(i - 1)
    last.wait_recv()
    scale = 1.0 / (torus.z * torus.flat * 16)
    for l in range(2):
        total = t_ref[l].astype(F32).reshape(ACC, F) * scale
        mix_sum[l] = total[:HALF]
        lcb_sum[l] = total[HALF:F]
        proj_sum[l] = total[F : F + K]
        out_sum[l] = total[F + K :, :E]
        gain_sum[l : l + 1] = jnp.concatenate([total[F + K + k : F + K + k + 1, E:] for k in range(3)], axis=1)
    finish(torus.y - 2)
    swap_b(torus.y - 1)
    finish(torus.y - 1)
    last.wait_send()
    for i in range(torus.y):
        swaps[i].wait_send()
        swaps_b[i].wait_send()
    pair.wait_send()
    for sem in (z_send, zb_send):
        take(spare.at[pl.ds(0, (torus.z - 1) * torus.y * torus.x)], sem)
    for sem in (f_send, fb_send):
        take(spare.at[pl.ds(0, (torus.flat - 1) * torus.z)], sem)
    take(x_parts.at[pl.ds(0, torus.x - 1)], g_send.at[1])
    take(g_spare.at[pl.ds(0, torus.y - 1)], g_send.at[2])
    take(g_spare.at[pl.ds(0, torus.z - 1)], g_send.at[3])
    take(g_spare.at[pl.ds(0, torus.y - 1)], g_send.at[4])
    take(x_full.at[pl.ds(0, torus.x - 1)], g_send.at[5])


def shards(torus, pooled, owner_order, fm_proj, fm_mix, fm_out, lcb_weight, gain, cotangent):
    chips = torus.z * torus.flat
    shape = (torus.z_lo, torus.y, torus.z_hi, torus.x, 8, 128)
    both = shape[:4] + (2, 8, 128)
    middle = (torus.z_lo, torus.z_hi, torus.y, torus.x, 8, 128)
    whole = (ROWS, F, E)
    depth = ACC // torus.x
    half = (torus.x, depth, F)
    chunk = (16, F)
    vmem = pl.BlockSpec(memory_space=pltpu.VMEM)
    spare = max((torus.z - 1) * torus.y * torus.x, (torus.flat - 1) * torus.z)
    operands = (
        pooled.T, cotangent.reshape(ROWS, chips, 128).transpose(1, 0, 2), owner_order.reshape(1, F),
        fm_proj.transpose(0, 2, 1), fm_mix, fm_out, lcb_weight, gain,
    )
    y_tiles, d_turned, proj_sum, mix_sum, out_sum, lcb_sum, gain_sum = pl.pallas_call(
        functools.partial(step_kernel, torus),
        out_shape=(
            jax.ShapeDtypeStruct((chips, 8, 128), BF16),
            jax.ShapeDtypeStruct((64, chips * 16), BF16),
            jax.ShapeDtypeStruct((2, K, F), F32),
            jax.ShapeDtypeStruct((2, HALF, F), F32),
            jax.ShapeDtypeStruct((2, K, E), F32),
            jax.ShapeDtypeStruct((2, HALF, F), F32),
            jax.ShapeDtypeStruct((2, E), F32),
        ),
        in_specs=[pl.BlockSpec(memory_space=pl.ANY)] * 8,
        out_specs=[vmem] * 7,
        scratch_shapes=[pltpu.VMEM(a.shape, a.dtype) for a in operands]
        + [
            pltpu.VMEM((2,) + half, BF16),
            pltpu.VMEM(both, BF16),
            pltpu.VMEM(shape, BF16),
            pltpu.VMEM(shape, BF16),
            pltpu.VMEM(middle, BF16),
            pltpu.VMEM(shape, BF16),
            pltpu.VMEM((spare, 8, 128), BF16),
            pltpu.VMEM((chips * 8, 128), F32),
            pltpu.VMEM((F, F), BF16),
            pltpu.VMEM((F, F), BF16),
            pltpu.VMEM((F, F), BF16),
            pltpu.VMEM((F, F), BF16),
            pltpu.VMEM((2, HALF + K, F), BF16),
            pltpu.VMEM((2, F, HALF + K), BF16),
            pltpu.VMEM((2,) + whole, BF16),
            pltpu.VMEM((2,) + whole, F32),
            pltpu.VMEM((2, ROWS, F, 1), F32),
            pltpu.VMEM((2, ROWS, K, E), BF16),
            pltpu.VMEM((2, ROWS * K, F), BF16),
            pltpu.VMEM((2, ROWS * K, HALF), BF16),
            pltpu.VMEM((ROWS * K, HALF), BF16),
            pltpu.VMEM((ROWS * K, F), BF16),
            pltpu.VMEM((ROWS, HALF + K, E), BF16),
            pltpu.VMEM((ROWS, HALF, E), F32),
            pltpu.VMEM((ROWS, HALF, E), BF16),
            pltpu.VMEM(whole, BF16),
            pltpu.VMEM(whole, BF16),
            pltpu.VMEM(whole, BF16),
            pltpu.VMEM((ACC, F), F32),
            pltpu.VMEM(shape, BF16),
            pltpu.VMEM(middle, BF16),
            pltpu.VMEM(both, BF16),
            pltpu.VMEM((chips * 8, 128), F32),
            pltpu.VMEM((2,) + half, BF16),
            pltpu.VMEM((max(torus.y, torus.z) - 1,) + chunk, BF16),
            pltpu.VMEM(half, BF16),
            pltpu.VMEM(half, BF16),
            pltpu.VMEM(half, BF16),
            pltpu.VMEM((torus.y,) + chunk, BF16),
            pltpu.VMEM((torus.y,) + chunk, BF16),
            pltpu.VMEM(chunk, BF16),
            pltpu.VMEM((torus.z,) + chunk, BF16),
            pltpu.VMEM(chunk, BF16),
            pltpu.VMEM((torus.y,) + chunk, BF16),
            pltpu.VMEM(half[1:], BF16),
            pltpu.VMEM(half, BF16),
        ]
        + [DMA((torus.y,)), DMA((torus.y,)), DMA, DMA((torus.y,)), DMA, DMA((torus.y,))] * 2
        + [DMA((7,)), DMA((7,)), DMA((8,))],
        compiler_params=pltpu.CompilerParams(
            collective_id=0, has_side_effects=True, vmem_limit_bytes=56 * 1024 * 1024
        ),
        name="train_step",
    )(*operands)
    return (
        y_tiles.transpose(1, 0, 2).reshape(ROWS, F * E),
        d_turned.T,
        proj_sum.transpose(0, 2, 1),
        mix_sum,
        out_sum,
        lcb_sum,
        gain_sum,
    )


def solution(mesh):
    torus = Torus(6, mesh.shape["wide"] // 6, 2, mesh.shape["grp"] // 4)
    return jax.shard_map(
        functools.partial(shards, torus),
        mesh=mesh,
        in_specs=(P(None, ("wide", "grp")), P(), P(), P(), P(), P(), P(), P(("wide", "grp"), None)),
        out_specs=(P(("wide", "grp"), None), P(None, ("wide", "grp")), P(), P(), P(), P(), P()),
        check_vma=False,
    )
```

```python
import functools

import jax
import jax.numpy as jnp
from jax import lax
from jax.experimental import pallas as pl
from jax.experimental.pallas import tpu as pltpu
from jax.sharding import PartitionSpec as P

F = 256
E = 192
MESH = pl.DeviceIdType.MESH
BF16 = jnp.bfloat16
F32 = jnp.float32
DMA = pltpu.SemaphoreType.DMA


def wrap(value, size):
    return jnp.where(value >= size, value - size, value)


class Torus:
    def __init__(self, z_lo, y, z_hi, x):
        self.z_lo, self.y, self.z_hi, self.x = z_lo, y, z_hi, x
        self.z = z_lo * z_hi
        self.flat = y * x
        self.offsets = sorted(range(y), key=lambda o: -min(o, y - o))
        self.z_steps = sorted(range(1, self.z), key=lambda o: min(o, self.z - o))

    def place(self):
        wide, grp = lax.axis_index("wide"), lax.axis_index("grp")
        z_lo = lax.div(wide, self.y)
        z_hi = lax.div(grp, 2 * self.x)
        rest = grp - z_hi * 2 * self.x
        x = lax.div(rest, 2)
        return z_hi * self.z_lo + z_lo, wide - z_lo * self.y, x, rest - 2 * x

    def split(self, z):
        high = jnp.where(z >= self.z_lo, 1, 0)
        return z - high * self.z_lo, high

    def device(self, z, y, x, core):
        z_lo, z_hi = self.split(z)
        return (z_lo * self.y + y, z_hi * 2 * self.x + x * 2 + core)


def hello(torus):
    z, y, x, core = torus.place()
    barrier = pltpu.get_barrier_semaphore()

    def signal(where):
        pl.semaphore_signal(barrier, inc=1, device_id=where, device_id_type=MESH)

    signal(torus.device(z, y, x, 1 - core))
    for step in torus.z_steps:
        signal(torus.device(wrap(z + step, torus.z), y, x, core))
    for dy in torus.offsets:
        for dx in range(torus.x):
            if dy or dx:
                signal(torus.device(z, wrap(y + dy, torus.y), wrap(x + dx, torus.x), core))


def all_here(torus):
    pl.semaphore_wait(pltpu.get_barrier_semaphore(), torus.z + torus.flat - 1)


def remote(src, dst, send, recv, where):
    return pltpu.make_async_remote_copy(
        src_ref=src, dst_ref=dst, send_sem=send, recv_sem=recv, device_id=where, device_id_type=MESH
    )


def take(ref, sem):
    pltpu.make_async_copy(ref, ref, sem).wait()


def send_z(torus, i, src, middle, z_send, z_recv):
    z, y, x, core = torus.place()
    y_to = wrap(y + torus.offsets[i], torus.y)
    z_lo, z_hi = torus.split(z)
    landing = middle.at[z_lo, z_hi, y_to]
    pltpu.make_async_copy(src.at[z_lo, y_to, z_hi], landing, z_recv.at[i]).start()
    for step in torus.z_steps:
        z_to = wrap(z + step, torus.z)
        lo_to, hi_to = torus.split(z_to)
        block = src.at[lo_to, y_to, hi_to]
        remote(block, landing, z_send, z_recv.at[i], torus.device(z_to, y, x, core)).start()


def send_flat(torus, i, middle, out, f_send, f_recv, z_recv):
    z, y, x, core = torus.place()
    y_to = wrap(y + torus.offsets[i], torus.y)
    take(middle.at[:, :, y_to], z_recv.at[i])
    for dx in range(torus.x):
        x_to = wrap(x + dx, torus.x)
        block = middle.at[:, :, y_to, x_to]
        if torus.offsets[i] == 0 and dx == 0:
            pltpu.make_async_copy(block, out(y, x), f_recv.at[i]).start()
        else:
            remote(block, out(y, x), f_send, f_recv.at[i], torus.device(z, y_to, x_to, core)).start()


NT = (((1,), (1,)), ((), ()))
TN = (((0,), (0,)), ((), ()))
NN = (((1,), (0,)), ((), ()))
K = 32
HALF = 128
ROWS = 8
ACC = 2 * HALF + 2 * K


def dot(left, right, dims):
    return lax.dot_general(left, right, dims, preferred_element_type=F32)


def read_rows(tiles, b):
    first, middle, last = (tiles[pl.ds(8 * j + b, HALF, stride=24), :] for j in range(3))
    even = jnp.concatenate([first, middle[:, :64]], axis=1)
    odd = jnp.concatenate([middle[:, 64:], last], axis=1)
    return jnp.concatenate([even, odd], axis=0).astype(BF16)


def write_rows(tiles, b, rows):
    even, odd = rows[:HALF], rows[HALF:]
    parts = (even[:, :128], jnp.concatenate([even[:, 128:], odd[:, :64]], axis=1), odd[:, 64:])
    for j, part in enumerate(parts):
        tiles[pl.ds(8 * j + b, HALF, stride=24), :] = part


PLAN = [
    "z0", "z1", "z2", "a0", "a1", "a2", "z3", "z4", "z5", "z6", "z7", "f0", "f1", "f2", "y0", "y1", "a3", "y2", "y3",
    "f3", "y4", "a4", "y5", "f4", "f5", "a5", "y6", "f6", "y7", "f7",
]


def step_kernel(
    torus,
    p_far, cot_far, order_far, proj_far, mix_far, out_far, lcb_far, gain_far,
    y_ref, d_ref, proj_sum, mix_sum, out_sum, lcb_sum, gain_sum,
    p_ref, cot_ref, order_ref, proj_ref, mix_ref, out_ref, lcb_ref, gain_ref, t_ref,
    pieces, inbox, src, middle, landed, spare,
    tiles, chosen, chosen_t, spread, spread_t, front, front_t, x_in, normed, inv, z_t, m_t, q_t, gq_t, gi_t, stack,
    lcb_rows, fm_rows, cot_top, cot_mid, y_rows, acc,
    leaving, middle_b, pieces_b, y_tiles, g_ref, g_spare, g_inbox, g_half, x_parts, x_own, y_parts, y_own, z_parts,
    g_done, y_full, y_dense, x_full,
    c_send, c_recv, z_send, z_recv, f_send, f_recv,
    cb_send, cb_recv, zb_send, zb_recv, fb_send, fb_recv, g_send, g_recv, near,
):
    z, y, x, core = torus.place()
    mate = torus.device(z, y, x, 1 - core)
    run = torus.z_hi * torus.x * 16
    block_rows = torus.z_hi * torus.x * 8
    far = (p_far, cot_far, order_far, proj_far, mix_far, out_far, lcb_far, gain_far)
    here = (p_ref, cot_ref, order_ref, proj_ref, mix_ref, out_ref, lcb_ref, gain_ref)
    loads = [pltpu.make_async_copy(a, b, near.at[k]) for k, (a, b) in enumerate(zip(far, here))]
    for load in loads:
        load.start()
    hello(torus)

    def prepare(i):
        y_to = wrap(y + torus.offsets[i], torus.y)

        def turn(z_lo, _):
            start = pl.multiple_of((z_lo * torus.y + y_to) * run, run)
            block = p_ref[:, pl.ds(start, run)].astype(F32)
            block = jnp.concatenate([block, block], axis=0).T.astype(BF16)
            pieces[z_lo, y_to] = block.reshape(torus.z_hi, torus.x, 2, 8, 128)
            return 0

        lax.fori_loop(0, torus.z_lo, turn, 0)

    swaps = []

    def swap(i):
        y_to = wrap(y + torus.offsets[i], torus.y)
        swaps.append(remote(
            pieces.at[:, y_to, :, :, 1 - core], inbox.at[:, y_to], c_send.at[i], c_recv.at[i], mate
        ))
        swaps[i].start()

    lanes = lax.broadcasted_iota(jnp.int32, (torus.x, 8, 128), 2)
    mine = jnp.where(lanes >= 64, 1, 0) == core

    def merge(i):
        y_to = wrap(y + torus.offsets[i], torus.y)
        swaps[i].wait_recv()

        def join(z_lo, _):
            for z_hi in range(torus.z_hi):
                own = pieces[z_lo, y_to, z_hi, :, core].astype(F32)
                other = inbox[z_lo, y_to, z_hi].astype(F32)
                src[z_lo, y_to, z_hi] = jnp.where(mine, own, other).astype(BF16)
            return 0

        lax.fori_loop(0, torus.z_lo, join, 0)
        send_z(torus, i, src, middle, z_send, z_recv)

    def onward(i):
        send_flat(torus, i, middle, lambda y, x: landed.at[:, y, :, x], f_send, f_recv, z_recv)

    loads[0].wait()
    prepare(0)
    all_here(torus)
    swap(0)
    prepare(1)
    swap(1)
    for i in range(torus.y):
        merge(i)
        if i + 2 < torus.y:
            prepare(i + 2)
            swap(i + 2)
        else:
            onward(i + 2 - torus.y)

    for load in loads[1:]:
        load.wait()
    spots = lax.broadcasted_iota(jnp.int32, (F, F), 0)
    places = lax.broadcasted_iota(jnp.int32, (F, F), 1)
    apart = (spots == jnp.where(places >= HALF, 2 * places - F + 1, 2 * places)).astype(F32)
    spread[...] = apart.astype(BF16)
    spread_t[...] = apart.T.astype(BF16)
    match = dot((spots == order_ref[...]).astype(BF16), spread[...], NN)
    chosen[...] = match.astype(BF16)
    chosen_t[...] = match.T.astype(BF16)
    for l in range(2):
        front[l, :HALF] = lcb_ref[l]
        front[l, HALF:] = proj_ref[l]
        front_t[l, :, :HALF] = lcb_ref[l].astype(F32).T.astype(BF16)
        front_t[l, :, HALF:] = proj_ref[l].astype(F32).T.astype(BF16)

    def open_cot(k, _):
        rows = cot_ref[pl.ds(8 * k, 8)].astype(F32).reshape(64, 128)
        tiles[pl.ds(pl.multiple_of(64 * k, 64), 64), :] = rows
        return 0

    lax.fori_loop(0, torus.z * torus.flat // 8, open_cot, 0)
    for i in range(torus.y):
        if i >= 2:
            onward(i)
        cot_top[i] = dot(spread[...], read_rows(tiles, i), NN).astype(BF16)
    for i in range(torus.y):
        y_from = wrap(y - torus.offsets[i] + torus.y, torus.y)
        take(landed.at[:, y_from], f_recv.at[i])

        def open_rows(z_lo, _):
            start = pl.multiple_of((z_lo * torus.y + y_from) * block_rows, block_rows)
            tiles[pl.ds(start, block_rows), :] = landed[z_lo, y_from].astype(F32).reshape(block_rows, 128)
            return 0

        lax.fori_loop(0, torus.z_lo, open_rows, 0)

    for b in range(ROWS):
        x_in[0, b] = dot(chosen[...], read_rows(tiles, b), NN).astype(BF16)
    for l in range(2):
        for b in range(ROWS):
            mixed = dot(front[l], x_in[l, b], NN)
            lcb_rows[b] = mixed[:HALF]
            z_t[l, b] = mixed[HALF:].astype(BF16)
        for b in range(ROWS):
            m_t[l, K * b : K * (b + 1)] = dot(z_t[l, b], x_in[l, b], NT).astype(BF16)
        q_t[l] = dot(m_t[l], mix_ref[l], NT).astype(BF16)
        for b in range(ROWS):
            for half in range(2):
                rows = slice(half * HALF, (half + 1) * HALF)
                branch = lcb_rows[b] if half else dot(q_t[l, K * b : K * (b + 1)], out_ref[l], TN)
                summed = branch + x_in[l, b, rows].astype(F32)
                center = summed - jnp.sum(summed, axis=-1, keepdims=True) * (1.0 / E)
                variance = jnp.sum(center * center, axis=-1, keepdims=True) * (1.0 / E)
                scale = lax.rsqrt(variance + 1e-05)
                inv[l, b, rows] = scale
                value = center * scale
                normed[l, b, rows] = value
                result = (value * gain_ref[l : l + 1]).astype(BF16)
                if l == 0:
                    x_in[1, b, rows] = result
                else:
                    y_rows[b, rows] = result

    pair = remote(g_ref.at[1 - core], g_inbox, g_send.at[0], g_recv.at[0], mate)
    share = g_ref.shape[2] // torus.y
    for l in (1, 0):
        gain_total = jnp.zeros((8, E), F32)
        for b in range(ROWS):
            for half in range(2):
                rows = slice(half * HALF, (half + 1) * HALF)
                cot = (cot_top if l else cot_mid)[b, rows].astype(F32)
                value = normed[l, b, rows]
                gain_total += jnp.sum((cot * value).reshape(HALF // 8, 8, E), axis=0)
                d_norm = cot * gain_ref[l : l + 1]
                mean = jnp.sum(d_norm, axis=-1, keepdims=True) * (1.0 / E)
                along = jnp.sum(d_norm * value, axis=-1, keepdims=True) * (1.0 / E)
                grad = (inv[l, b, rows] * (d_norm - mean - value * along)).astype(BF16)
                if half:
                    stack[b, :HALF] = grad
                else:
                    fm_rows[b] = grad
        for b in range(ROWS):
            gq_t[K * b : K * (b + 1)] = dot(out_ref[l], fm_rows[b], NT).astype(BF16)
        gi_t[...] = dot(gq_t[...], mix_ref[l], NN).astype(BF16)
        acc[:HALF] = dot(gq_t[...], m_t[l], TN)
        out_total = jnp.zeros((K, E), F32)
        for b in range(ROWS):
            out_total += dot(q_t[l, K * b : K * (b + 1)], fm_rows[b], NN)
            stack[b, HALF:] = dot(gi_t[K * b : K * (b + 1)], x_in[l, b], NN).astype(BF16)
        front_total = jnp.zeros((HALF + K, F), F32)
        for b in range(ROWS):
            front_total += dot(stack[b], x_in[l, b], NT)
        acc[2 * HALF : 2 * HALF + K] = front_total[HALF:]
        acc[HALF : 2 * HALF] = front_total[:HALF]
        gain_row = jnp.sum(gain_total, axis=0, keepdims=True)
        acc[K + 2 * HALF :, :E] = out_total
        acc[K + 2 * HALF :, E:] = jnp.zeros((K, F - E), F32)
        for part in range(3):
            acc[K + 2 * HALF + part : K + 2 * HALF + part + 1, E:] = gain_row[:, part * 64 : (part + 1) * 64]
        for k in range(torus.x):
            depth = torus.y * share
            g_ref[l, k] = acc[k * depth : (k + 1) * depth].astype(BF16)
        if l == 0:
            pair.start()
        for b in range(ROWS):
            total = dot(front_t[l], stack[b], NN) + dot(gi_t[K * b : K * (b + 1)], z_t[l, b], TN)
            total += jnp.concatenate([fm_rows[b], stack[b, :HALF]], axis=0).astype(F32)
            cot_mid[b] = total.astype(BF16)
    for b in range(ROWS):
        write_rows(tiles, b, dot(chosen_t[...], cot_mid[b], NN))

    def leave(i):
        y_to = wrap(y + torus.offsets[i], torus.y)

        def close(z_lo, _):
            start = pl.multiple_of((z_lo * torus.y + y_to) * block_rows, block_rows)
            rows = tiles[pl.ds(start, block_rows), :].reshape(torus.z_hi, torus.x, 8, 128)
            leaving[z_lo, y_to] = rows.astype(BF16)
            return 0

        lax.fori_loop(0, torus.z_lo, close, 0)
        send_z(torus, i, leaving, middle_b, zb_send, zb_recv)

    def along_x(block, landing, k):
        pltpu.make_async_copy(block(x), landing, g_recv.at[k]).start()
        for dx in range(1, torus.x):
            x_to = wrap(x + dx, torus.x)
            remote(block(x_to), landing, g_send.at[k], g_recv.at[k], torus.device(z, y, x_to, core)).start()

    def along_y(block, landing, k):
        pltpu.make_async_copy(block(y), landing, g_recv.at[k]).start()
        for dy in range(1, torus.y):
            y_to = wrap(y + dy, torus.y)
            remote(block(y_to), landing, g_send.at[k], g_recv.at[k], torus.device(z, y_to, x, core)).start()

    def sum_pair():
        pair.wait_recv()

        def add(k, _):
            g_half[k] = (g_ref[core, k].astype(F32) + g_inbox[k].astype(F32)).astype(BF16)
            return 0

        lax.fori_loop(0, torus.x, add, 0)
        along_x(lambda x_to: g_half.at[x_to], x_parts.at[x], 1)

    def sum_x():
        take(x_parts, g_recv.at[1])
        total = jnp.sum(x_parts[...].astype(F32), axis=0)
        rest = jnp.zeros((16 - share, F), F32)
        for k in range(torus.y):
            x_own[k] = jnp.concatenate([total[k * share : (k + 1) * share], rest], axis=0).astype(BF16)
        along_y(lambda y_to: x_own.at[y_to], y_parts.at[y], 2)

    def sum_y():
        take(y_parts, g_recv.at[2])
        y_own[...] = jnp.sum(y_parts[...].astype(F32), axis=0).astype(BF16)
        landing = z_parts.at[z]
        pltpu.make_async_copy(y_own, landing, g_recv.at[3]).start()
        for step in torus.z_steps:
            where = torus.device(wrap(z + step, torus.z), y, x, core)
            remote(y_own, landing, g_send.at[3], g_recv.at[3], where).start()

    def sum_z():
        take(z_parts, g_recv.at[3])
        g_done[...] = jnp.sum(z_parts[...].astype(F32), axis=0).astype(BF16)
        along_y(lambda y_to: g_done, y_full.at[y], 4)

    def share_x():
        take(y_full, g_recv.at[4])
        y_dense[...] = jnp.concatenate(
            [y_full[k].astype(F32)[:share] for k in range(torus.y)], axis=0
        ).astype(BF16)
        along_x(lambda x_to: y_dense, x_full.at[x], 5)

    last = remote(x_full, t_ref.at[core], g_send.at[6], g_recv.at[6], mate)

    def share_pair():
        take(x_full, g_recv.at[5])
        last.start()
        t_ref[core] = x_full[...]

    parts = [sum_pair, sum_x, sum_y, sum_z, share_x, share_pair]
    for step in PLAN:
        kind, i = step[0], int(step[1:])
        if kind == "a":
            parts[i]()
        elif kind == "z":
            leave(i)
        elif kind == "y":
            write_rows(y_tiles, i, dot(spread_t[...], y_rows[i], NN))
        else:
            send_flat(torus, i, middle_b, lambda y, x: pieces_b.at[:, y, :, x, core], fb_send, fb_recv, zb_recv)

    def close_y(k, _):
        rows = y_tiles[pl.ds(pl.multiple_of(64 * k, 64), 64), :].reshape(8, 8, 128)
        y_ref[pl.ds(8 * k, 8)] = rows.astype(BF16)
        return 0

    lax.fori_loop(0, torus.z * torus.flat // 8, close_y, 0)
    swaps_b = []

    def swap_b(i):
        y_from = wrap(y - torus.offsets[i] + torus.y, torus.y)
        block = pieces_b.at[:, y_from, :, :, core]
        take(block, fb_recv.at[i])
        swaps_b.append(remote(block, block, cb_send.at[i], cb_recv.at[i], mate))
        swaps_b[i].start()

    def finish(i):
        y_from = wrap(y - torus.offsets[i] + torus.y, torus.y)
        swaps_b[i].wait_recv()

        def turn(z_lo, _):
            start = pl.multiple_of((z_lo * torus.y + y_from) * run, run)
            block = pieces_b[z_lo, y_from].astype(F32).reshape(run, 128).T
            d_ref[:, pl.ds(start, run)] = jnp.where(core == 0, block[:64], block[64:]).astype(BF16)
            return 0

        lax.fori_loop(0, torus.z_lo, turn, 0)

    for i in range(torus.y - 1):
        swap_b(i)
        if i:
            finish(i - 1)
    last.wait_recv()
    scale = 1.0 / (torus.z * torus.flat * 16)
    for l in range(2):
        total = t_ref[l].astype(F32).reshape(ACC, F) * scale
        mix_sum[l] = total[:HALF]
        lcb_sum[l] = total[HALF:F]
        proj_sum[l] = total[F : F + K]
        out_sum[l] = total[F + K :, :E]
        gain_sum[l : l + 1] = jnp.concatenate([total[F + K + k : F + K + k + 1, E:] for k in range(3)], axis=1)
    finish(torus.y - 2)
    swap_b(torus.y - 1)
    finish(torus.y - 1)
    last.wait_send()
    for i in range(torus.y):
        swaps[i].wait_send()
        swaps_b[i].wait_send()
    pair.wait_send()
    for sem in (z_send, zb_send):
        take(spare.at[pl.ds(0, (torus.z - 1) * torus.y * torus.x)], sem)
    for sem in (f_send, fb_send):
        take(spare.at[pl.ds(0, (torus.flat - 1) * torus.z)], sem)
    take(x_parts.at[pl.ds(0, torus.x - 1)], g_send.at[1])
    take(g_spare.at[pl.ds(0, torus.y - 1)], g_send.at[2])
    take(g_spare.at[pl.ds(0, torus.z - 1)], g_send.at[3])
    take(g_spare.at[pl.ds(0, torus.y - 1)], g_send.at[4])
    take(x_full.at[pl.ds(0, torus.x - 1)], g_send.at[5])


def hand_over_kernel(*refs):
    count = len(refs) // 2
    sems = refs[-1]
    copies = []
    for source, target in zip(refs[:count], refs[count : 2 * count]):
        pieces = 4 if source.dtype == BF16 else 1
        size = source.shape[0] // pieces
        for k in range(pieces):
            rows = pl.ds(k * size, size)
            copies.append(pltpu.make_async_copy(source.at[rows], target.at[rows], sems.at[len(copies)]))
    for copy in copies:
        copy.start()
    for copy in copies:
        copy.wait()


def hand_over(arrays):
    anywhere = pl.BlockSpec(memory_space=pl.ANY)
    return pl.pallas_call(
        hand_over_kernel,
        out_shape=tuple(jax.ShapeDtypeStruct(a.shape, a.dtype) for a in arrays),
        in_specs=[anywhere] * len(arrays),
        out_specs=[anywhere] * len(arrays),
        scratch_shapes=[DMA((4 * len(arrays),))],
        compiler_params=pltpu.CompilerParams(vmem_limit_bytes=56 * 1024 * 1024),
        name="hand_over",
    )(*arrays)


def shards(torus, pooled, owner_order, fm_proj, fm_mix, fm_out, lcb_weight, gain, cotangent):
    chips = torus.z * torus.flat
    shape = (torus.z_lo, torus.y, torus.z_hi, torus.x, 8, 128)
    both = shape[:4] + (2, 8, 128)
    middle = (torus.z_lo, torus.z_hi, torus.y, torus.x, 8, 128)
    whole = (ROWS, F, E)
    depth = ACC // torus.x
    half = (torus.x, depth, F)
    chunk = (16, F)
    vmem = pl.BlockSpec(memory_space=pltpu.VMEM)
    spare = max((torus.z - 1) * torus.y * torus.x, (torus.flat - 1) * torus.z)
    operands = (
        pooled.T, cotangent.reshape(ROWS, chips, 128).transpose(1, 0, 2), owner_order.reshape(1, F),
        fm_proj.transpose(0, 2, 1), fm_mix, fm_out, lcb_weight, gain,
    )
    results = pl.pallas_call(
        functools.partial(step_kernel, torus),
        out_shape=(
            jax.ShapeDtypeStruct((chips, 8, 128), BF16),
            jax.ShapeDtypeStruct((64, chips * 16), BF16),
            jax.ShapeDtypeStruct((2, K, F), F32),
            jax.ShapeDtypeStruct((2, HALF, F), F32),
            jax.ShapeDtypeStruct((2, K, E), F32),
            jax.ShapeDtypeStruct((2, HALF, F), F32),
            jax.ShapeDtypeStruct((2, E), F32),
        ),
        in_specs=[pl.BlockSpec(memory_space=pl.ANY)] * 8,
        out_specs=[vmem] * 7,
        scratch_shapes=[pltpu.VMEM(a.shape, a.dtype) for a in operands]
        + [
            pltpu.VMEM((2,) + half, BF16),
            pltpu.VMEM(both, BF16),
            pltpu.VMEM(shape, BF16),
            pltpu.VMEM(shape, BF16),
            pltpu.VMEM(middle, BF16),
            pltpu.VMEM(shape, BF16),
            pltpu.VMEM((spare, 8, 128), BF16),
            pltpu.VMEM((chips * 8, 128), F32),
            pltpu.VMEM((F, F), BF16),
            pltpu.VMEM((F, F), BF16),
            pltpu.VMEM((F, F), BF16),
            pltpu.VMEM((F, F), BF16),
            pltpu.VMEM((2, HALF + K, F), BF16),
            pltpu.VMEM((2, F, HALF + K), BF16),
            pltpu.VMEM((2,) + whole, BF16),
            pltpu.VMEM((2,) + whole, F32),
            pltpu.VMEM((2, ROWS, F, 1), F32),
            pltpu.VMEM((2, ROWS, K, E), BF16),
            pltpu.VMEM((2, ROWS * K, F), BF16),
            pltpu.VMEM((2, ROWS * K, HALF), BF16),
            pltpu.VMEM((ROWS * K, HALF), BF16),
            pltpu.VMEM((ROWS * K, F), BF16),
            pltpu.VMEM((ROWS, HALF + K, E), BF16),
            pltpu.VMEM((ROWS, HALF, E), F32),
            pltpu.VMEM((ROWS, HALF, E), BF16),
            pltpu.VMEM(whole, BF16),
            pltpu.VMEM(whole, BF16),
            pltpu.VMEM(whole, BF16),
            pltpu.VMEM((ACC, F), F32),
            pltpu.VMEM(shape, BF16),
            pltpu.VMEM(middle, BF16),
            pltpu.VMEM(both, BF16),
            pltpu.VMEM((chips * 8, 128), F32),
            pltpu.VMEM((2,) + half, BF16),
            pltpu.VMEM((max(torus.y, torus.z) - 1,) + chunk, BF16),
            pltpu.VMEM(half, BF16),
            pltpu.VMEM(half, BF16),
            pltpu.VMEM(half, BF16),
            pltpu.VMEM((torus.y,) + chunk, BF16),
            pltpu.VMEM((torus.y,) + chunk, BF16),
            pltpu.VMEM(chunk, BF16),
            pltpu.VMEM((torus.z,) + chunk, BF16),
            pltpu.VMEM(chunk, BF16),
            pltpu.VMEM((torus.y,) + chunk, BF16),
            pltpu.VMEM(half[1:], BF16),
            pltpu.VMEM(half, BF16),
        ]
        + [DMA((torus.y,)), DMA((torus.y,)), DMA, DMA((torus.y,)), DMA, DMA((torus.y,))] * 2
        + [DMA((7,)), DMA((7,)), DMA((8,))],
        compiler_params=pltpu.CompilerParams(
            collective_id=0, has_side_effects=True, vmem_limit_bytes=56 * 1024 * 1024
        ),
        name="train_step",
    )(*operands)
    y_tiles, d_turned, proj_sum, mix_sum, out_sum, lcb_sum, gain_sum = hand_over(results)
    return (
        y_tiles.transpose(1, 0, 2).reshape(ROWS, F * E),
        d_turned.T,
        proj_sum.transpose(0, 2, 1),
        mix_sum,
        out_sum,
        lcb_sum,
        gain_sum,
    )


def solution(mesh):
    torus = Torus(6, mesh.shape["wide"] // 6, 2, mesh.shape["grp"] // 4)
    return jax.shard_map(
        functools.partial(shards, torus),
        mesh=mesh,
        in_specs=(P(None, ("wide", "grp")), P(), P(), P(), P(), P(), P(), P(("wide", "grp"), None)),
        out_specs=(P(("wide", "grp"), None), P(None, ("wide", "grp")), P(), P(), P(), P(), P()),
        check_vma=False,
    )
```
